32 devices in a mesh: tm: 2 (over y), gz: 4 (over z), row: 4 (over x, core).
Axes of the slice: x: 2, y: 2, z: 4, core: 2. Of those that a mesh axis runs over, the one named last changes fastest.
Arguments:
- starts: float32 [2, 6, 256, 2048], P('tm', None, 'row', 'gz'), may hold values from -6 to 6
- coarse_map: float32 [2, 36, 64, 512], P('tm', None, 'row', 'gz'), may hold values from -0.2 to 1, as said below
- diffusivity: float32 [6], replicated, may hold values from 0.5 to 1
Outputs:
- next_starts: float32 [2, 6, 256, 2048], P('tm', None, 'row', 'gz')
The draws below stay inside these ranges and needn't reach their ends.
Inputs may be any that keep to these rules, and one draw needn't show every extreme that they name: `coarse_map`: in every coarse cell the absolute values of each row of the matrix sum to at most 0.99; diagonal entries are positive.
All inputs are finite; a program needn't handle non-finite values.
Results may differ from the reference program's by a relative error of at most 0.0001.
Values sent between devices are 32-bit elements; how exact they have to be, the bound alone decides.
A program may use at most 64 MiB of HBM per device.

```python
import math
import jax
import jax.numpy as jnp
from jax import lax

FIELDS = 6
FSTEPS = 4
TIME_PARTITIONS = 2
NR = 256
NZ = 2048
NRC = 64
NZC = 512


def draw_coarse_map(key, part):
    random_key_list = jax.random.split(jax.random.fold_in(key, 17), 6)
    slow_count = 3
    order = jax.random.permutation(random_key_list[0], 6)
    sluggish_indicator = (order < slow_count)[None, :, None, None]
    base_slow = jax.random.uniform(random_key_list[1], (TIME_PARTITIONS, 6, 1, 1), jnp.float32, 0.96, 0.99)
    base_fast = jax.random.uniform(random_key_list[2], (TIME_PARTITIONS, 6, 1, 1), jnp.float32, 0.25, 0.55)
    cell_factor = jax.random.uniform(random_key_list[3], (TIME_PARTITIONS, 6, NRC, NZC), jnp.float32, 0.985, 1.0)
    surge_partitions = jax.random.randint(random_key_list[4], (2,), 0, TIME_PARTITIONS)
    surge_indicator = jnp.any(jnp.arange(TIME_PARTITIONS)[:, None] == surge_partitions[None, :], axis=1)[:, None, None, None]
    diagonal_entries = jnp.where(sluggish_indicator, base_slow, base_fast) * cell_factor
    diagonal_entries = diagonal_entries * jnp.where(jnp.logical_and(surge_indicator, sluggish_indicator), 0.7, 1.0)
    offset = jax.random.uniform(random_key_list[5], (TIME_PARTITIONS, 6, 6, NRC, NZC), jnp.float32, -1.0, 1.0)
    offset = offset * ((0.99 - diagonal_entries) / 5.0)[:, :, None]
    identity_matrix = jnp.eye(6, dtype=jnp.float32)[None, :, :, None, None]
    matrix = offset * (1.0 - identity_matrix) + identity_matrix * diagonal_entries[:, :, None]
    return matrix.reshape(TIME_PARTITIONS, 36, NRC, NZC)


def block_levels(own_key, dims, shards, low, top_value):
    def one(axis_at, blocks):
        steps = jax.random.uniform(jax.random.fold_in(jax.random.fold_in(own_key, 6), axis_at), (blocks,), jnp.float32, low / len(shards), top_value / len(shards))
        return jnp.repeat(jnp.exp(steps), dims[axis_at] // blocks).reshape((-1,) + (1,) * (len(dims) - axis_at - 1))

    loudness = one(*shards[0])
    for cut in shards[1:]:
        loudness = loudness * one(*cut)
    return loudness


def bell_draw(rng, shape, width, reach, cuts=(), kind=jnp.bfloat16):
    array = jax.random.normal(rng, shape, jnp.float32) * width
    if len(cuts) > 0:
        array = block_levels(rng, shape, cuts, -0.22, 0.18) * array
    return jnp.clip(array, min=-reach, max=reach).astype(kind)


def setup_inputs(seed: int = 0) -> dict:
    keys = jax.random.split(jax.random.key(seed), 4)
    starts = bell_draw(keys[0], (TIME_PARTITIONS, FIELDS, NR, NZ), 1.0, 6.0, ((0, 2), (2, 4), (3, 4)), jnp.float32)
    coarse_map = draw_coarse_map(jax.random.fold_in(keys[3], 71), 0)
    diffusivity = jnp.clip(jnp.exp(jax.random.uniform(keys[2], (FIELDS,), jnp.float32, math.log(0.5), math.log(1.0))), 0.5, 1.0)
    return {"starts": starts, "coarse_map": coarse_map, "diffusivity": diffusivity}


time_step = 0.24


def fine_step(padded, row_start, diffusivity):
    center = padded[:, 1:-1, 1:-1]
    height_rows = center.shape[1]
    speed = 0.25 * jnp.tanh(padded[1])
    east_cell = padded[:, 1:-1, 2:]
    west_cell = padded[:, 1:-1, :-2]
    north_cell = padded[:, 2:, 1:-1]
    south_cell = padded[:, :-2, 1:-1]
    speed_mid = speed[1:-1, 1:-1]
    eastward_flux = 0.25 * (speed_mid + speed[1:-1, 2:]) * (center + east_cell)
    flux_west = 0.25 * (speed_mid + speed[1:-1, :-2]) * (center + west_cell)
    radius = (row_start + jnp.arange(height_rows, dtype=jnp.int32)).astype(jnp.float32)[:, None]
    radial = ((radius + 1.0) * (north_cell - center) - radius * (center - south_cell)) / (radius + 0.5)
    spread_rate = diffusivity[:, None, None]
    change = spread_rate * (radial + east_cell - 2.0 * center + west_cell) - (eastward_flux - flux_west)
    return center + time_step * change


def restrict(field):
    count, height_rows, width_cols = field.shape
    return field.reshape(count, height_rows // 4, 4, width_cols // 4, 4).mean(axis=(2, 4))


def prolong(field):
    return jnp.repeat(jnp.repeat(field, 4, axis=1), 4, axis=2)


def apply_map(matrix, vector):
    return jnp.sum(matrix * vector[None], axis=1)


def reference(starts, coarse_map, diffusivity):
    later_starts = jnp.concatenate([starts[1:], jnp.zeros_like(starts[:1])], axis=0)

    def slice_turn(carry, inputs):
        start_state, later_state, matrix_flat = inputs
        matrix = matrix_flat.reshape(6, 6, matrix_flat.shape[1], matrix_flat.shape[2])

        def one_step(turn_index, state):
            padded = jnp.pad(state, ((0, 0), (1, 1), (1, 1)))
            return fine_step(padded, 0, diffusivity)

        fine_state = lax.fori_loop(0, FSTEPS, one_step, start_state)
        jump = restrict(fine_state) - restrict(later_state)
        mapped = apply_map(matrix, carry)
        result = fine_state + prolong(mapped)
        return mapped + jump, result

    carry_zero = jnp.zeros((FIELDS, NRC, NZC), jnp.float32)
    last_carry, outputs = lax.scan(slice_turn, carry_zero, (starts, later_starts, coarse_map))
    return outputs
```

```python
import functools

import jax
import jax.numpy as jnp
from jax import lax
from jax.experimental import pallas as pl
from jax.experimental.pallas import tpu as pltpu
from jax.sharding import PartitionSpec as P

FSTEPS = 4
TIME_STEP = 0.24
LANES = 128
PAD = 8
MESH = pl.DeviceIdType.MESH


def pieces(value):
    high = value.astype(jnp.bfloat16)
    low = (value - high.astype(jnp.float32)).astype(jnp.bfloat16)
    return high, low


def kernel(
    sizes, starts, coarse_map, diffusivity, out,
    state_a, state_b, packed, from_left, from_right, coef_a, coef_b, matrix,
    start_mean, gather, spread, outgoing, incoming,
    in_sem, map_sem, row_send, row_recv, col_send, col_recv, cor_send, cor_recv,
    carry_send, carry_recv, out_sem,
):
    slices, cols, rows = sizes
    fields, height, width = starts.shape
    tiles = width // LANES
    n, g, r = lax.axis_index("tm"), lax.axis_index("gz"), lax.axis_index("row")

    def load_tile(l):
        return pltpu.make_async_copy(
            starts.at[:, :, pl.ds(l * LANES, LANES)],
            state_a.at[:, l, pl.ds(PAD, height), :], in_sem.at[l])

    order = [0, tiles - 1] + list(range(1, tiles - 1))
    for l in order:
        load_tile(l).start()
    load_map = pltpu.make_async_copy(coarse_map, matrix, map_sem)
    load_map.start()

    up, down, left, right = r > 0, r < rows - 1, g > 0, g < cols - 1
    both = jnp.logical_and
    neighbours = [
        (up, {"row": r - 1}), (down, {"row": r + 1}),
        (left, {"gz": g - 1}), (right, {"gz": g + 1}),
        (both(up, left), {"row": r - 1, "gz": g - 1}),
        (both(up, right), {"row": r - 1, "gz": g + 1}),
        (both(down, left), {"row": r + 1, "gz": g - 1}),
        (both(down, right), {"row": r + 1, "gz": g + 1}),
        (n > 0, {"tm": n - 1}), (n < slices - 1, {"tm": n + 1}),
    ]
    barrier = pltpu.get_barrier_semaphore()
    present = 0
    for there, device in neighbours:
        present = present + there.astype(jnp.int32)

        @pl.when(there)
        def _(device=device):
            pl.semaphore_signal(barrier, inc=1, device_id=device, device_id_type=MESH)

    blank_rows = jnp.zeros((fields, tiles, PAD, LANES), jnp.float32)
    blank_tile = jnp.zeros((PAD, LANES), jnp.float32)
    bottom = PAD + height

    @pl.when(jnp.logical_not(up))
    def _():
        state_a[:, :tiles, 0:PAD, :] = blank_rows

    @pl.when(jnp.logical_not(down))
    def _():
        state_a[:, :tiles, bottom:, :] = blank_rows

    for ref, side in ((from_left, left), (from_right, right)):
        @pl.when(jnp.logical_not(both(side, up)))
        def _(ref=ref):
            ref[0:PAD, :] = blank_tile

        @pl.when(jnp.logical_not(both(side, down)))
        def _(ref=ref):
            ref[bottom:, :] = blank_tile

        @pl.when(jnp.logical_not(side))
        def _(ref=ref):
            ref[pl.ds(PAD, height), :] = jnp.zeros((height, LANES), jnp.float32)

    lane8 = lax.broadcasted_iota(jnp.int32, (8, LANES), 1)
    lane_all = lax.broadcasted_iota(jnp.int32, (height, LANES), 1)

    load_tile(0).wait()
    load_tile(tiles - 1).wait()
    pack = jnp.zeros((height, LANES), jnp.float32)
    for f in range(fields):
        edges = jnp.where(lane_all < 64, state_a[f, 0, pl.ds(PAD, height), :],
                          state_a[f, tiles - 1, pl.ds(PAD, height), :])
        pack = jnp.where(lane_all // 8 == f, pltpu.roll(edges, 8 * f + 4, 1), pack)
    packed[...] = pack

    pl.semaphore_wait(barrier, present)

    def row_copy(l, way):
        source = pl.ds(0, PAD) if way == 0 else pl.ds(height - PAD, PAD)
        target = pl.ds(bottom, PAD) if way == 0 else pl.ds(0, PAD)
        return pltpu.make_async_remote_copy(
            src_ref=starts.at[:, source, pl.ds(l * LANES, LANES)],
            dst_ref=state_a.at[:, l, target, :],
            send_sem=row_send.at[way, l], recv_sem=row_recv.at[way, l],
            device_id={"row": r - 1 if way == 0 else r + 1}, device_id_type=MESH)

    def col_copy(way):
        return pltpu.make_async_remote_copy(
            src_ref=packed,
            dst_ref=(from_right if way == 0 else from_left).at[pl.ds(PAD, height), :],
            send_sem=col_send.at[way], recv_sem=col_recv.at[way],
            device_id={"gz": g - 1 if way == 0 else g + 1}, device_id_type=MESH)

    def cor_copy(v, h):
        source = pl.ds(0, PAD) if v == 0 else pl.ds(height - PAD, PAD)
        target = pl.ds(bottom, PAD) if v == 0 else pl.ds(0, PAD)
        return pltpu.make_async_remote_copy(
            src_ref=packed.at[source, :],
            dst_ref=(from_right if h == 0 else from_left).at[target, :],
            send_sem=cor_send.at[v, h], recv_sem=cor_recv.at[v, h],
            device_id={"row": r - 1 if v == 0 else r + 1, "gz": g - 1 if h == 0 else g + 1},
            device_id_type=MESH)

    transfers = [
        (left, right, [col_copy(0)]),
        (right, left, [col_copy(1)]),
        (both(up, left), both(down, right), [cor_copy(0, 0)]),
        (both(up, right), both(down, left), [cor_copy(0, 1)]),
        (both(down, left), both(up, right), [cor_copy(1, 0)]),
        (both(down, right), both(up, left), [cor_copy(1, 1)]),
        (up, down, [row_copy(l, 0) for l in range(tiles)]),
        (down, up, [row_copy(l, 1) for l in range(tiles)]),
    ]
    for sends, _, copies in transfers:
        @pl.when(sends)
        def _(copies=copies):
            for copy in copies:
                copy.start()

    full = height + 2 * PAD
    grow = r * height - PAD + lax.broadcasted_iota(jnp.int32, (full, LANES), 0)
    radius = grow.astype(jnp.float32)
    inside = both(grow >= 0, grow < rows * height)
    coef_a[...] = jnp.where(inside, (radius + 1.0) / (radius + 0.5), 0.0)
    coef_b[...] = jnp.where(inside, radius / (radius + 0.5), 0.0)

    coarse_cols = width // 4
    fine_at = lax.broadcasted_iota(jnp.int32, (width, coarse_cols), 0)
    coarse_at = lax.broadcasted_iota(jnp.int32, (width, coarse_cols), 1)
    gather[...] = jnp.where(fine_at // 4 == coarse_at, 1.0, 0.0).astype(jnp.bfloat16)
    fine_at = lax.broadcasted_iota(jnp.int32, (coarse_cols, width), 1)
    coarse_at = lax.broadcasted_iota(jnp.int32, (coarse_cols, width), 0)
    spread[...] = jnp.where(fine_at // 4 == coarse_at, 1.0, 0.0).astype(jnp.bfloat16)

    coarse_rows = height // 4

    def restrict(ref):
        total = jnp.zeros((fields * coarse_rows, coarse_cols), jnp.float32)
        for l in range(tiles):
            sums = []
            for f in range(fields):
                part = [ref[f, l, pl.ds(PAD + k, coarse_rows, stride=4), :] for k in range(4)]
                sums.append((part[0] + part[1]) + (part[2] + part[3]))
            high, low = pieces(jnp.concatenate(sums, axis=0))
            pick = gather[pl.ds(l * LANES, LANES), :]
            total = total + jnp.dot(high, pick, preferred_element_type=jnp.float32)
            total = total + jnp.dot(low, pick, preferred_element_type=jnp.float32)
        return total * 0.0625

    for l in range(1, tiles - 1):
        load_tile(l).wait()

    @pl.when(n > 0)
    def _():
        start_mean[...] = restrict(state_a)

    for _, receives, copies in transfers:
        @pl.when(receives)
        def _(copies=copies):
            for copy in copies:
                copy.wait_recv()

    lane_full = lax.broadcasted_iota(jnp.int32, (full, LANES), 1)
    merged = jnp.where(lane_full % 8 < 4, from_left[...], from_right[...])
    edge = jnp.logical_or(lane_full < 4, lane_full >= LANES - 4)
    for f in range(fields):
        state_a[f, tiles] = jnp.where(edge, pltpu.roll(merged, LANES - 8 * f - 4, 1), 0.0)

    keep = jnp.logical_or(both(lane8 < 64, right), both(lane8 >= 64, left))
    first, final = lane8 == 0, lane8 == LANES - 1

    def shifted(tiles_of, wanted):
        count = len(tiles_of)
        east = [pltpu.roll(x, LANES - 1, 1) for x in tiles_of]
        west = [pltpu.roll(x, 1, 1) for x in tiles_of]
        return ([jnp.where(final, east[(l + 1) % count], east[l]) for l in range(wanted)],
                [jnp.where(first, west[l - 1], west[l]) for l in range(wanted)])

    rates = [TIME_STEP * diffusivity[f] for f in range(fields)]

    def fine_step(source, target, begin, windows, wanted):
        def body(k, _):
            at = begin + 8 * k
            here = pl.ds(at, 8)
            speed = [jnp.tanh(source[1, l, here, :]) for l in range(tiles + 1)]
            turned = [pltpu.roll(x, LANES - 1, 1) for x in speed]
            flux = [(0.0625 * TIME_STEP) * (speed[l] + jnp.where(
                final, turned[(l + 1) % (tiles + 1)], turned[l])) for l in range(tiles + 1)]
            turned = [pltpu.roll(x, 1, 1) for x in flux]
            flux_west = [jnp.where(first, turned[l - 1], turned[l]) for l in range(wanted)]
            gain = [flux_west[l] - flux[l] for l in range(wanted)]
            a, b = coef_a[here, :], coef_b[here, :]
            for f in range(fields):
                rate = rates[f]
                a_f, b_f = rate * a, rate * b
                middle = 1.0 - 4.0 * rate
                center = [source[f, l, here, :] for l in range(tiles + 1)]
                east, west = shifted(center, wanted)
                for l in range(wanted):
                    new = (
                        center[l] * (middle + gain[l])
                        + east[l] * (rate - flux[l])
                        + west[l] * (rate + flux_west[l])
                        + (a_f * source[f, l, pl.ds(at + 1, 8), :]
                           + b_f * source[f, l, pl.ds(at - 1, 8), :])
                    )
                    if l == tiles:
                        new = jnp.where(keep, new, 0.0)
                    target[f, l, here, :] = new
            return 0

        lax.fori_loop(0, windows, body, 0)

    source, target = state_a, state_b
    for turn in range(FSTEPS):
        if turn < FSTEPS - 1:
            fine_step(source, target, PAD - FSTEPS, (height + 2 * FSTEPS) // 8, tiles + 1)
        else:
            fine_step(source, target, PAD, height // 8, tiles)
        source, target = target, source
    fine = source

    load_map.wait()

    carry_copy = pltpu.make_async_remote_copy(
        src_ref=outgoing, dst_ref=incoming, send_sem=carry_send, recv_sem=carry_recv,
        device_id={"tm": n + 1}, device_id_type=MESH)

    def send_out(f, l):
        return pltpu.make_async_copy(
            fine.at[f, l, pl.ds(PAD, height), :],
            out.at[f, :, pl.ds(l * LANES, LANES)], out_sem.at[f, l])

    @pl.when(n == 0)
    def _():
        for f in range(fields):
            for l in range(tiles):
                send_out(f, l).start()

        @pl.when(n < slices - 1)
        def _():
            outgoing[...] = restrict(fine)
            carry_copy.start()

    @pl.when(n > 0)
    def _():
        @pl.when(n < slices - 1)
        def _():
            outgoing[...] = restrict(fine)

        carry_copy.wait_recv()
        carry = incoming[...] - start_mean[...]
        mapped = []
        for f in range(fields):
            total = jnp.zeros((coarse_rows, coarse_cols), jnp.float32)
            for h in range(fields):
                total = total + matrix[f * fields + h] * carry[h * coarse_rows:(h + 1) * coarse_rows]
            mapped.append(total)
        mapped = jnp.concatenate(mapped, axis=0)

        @pl.when(n < slices - 1)
        def _():
            outgoing[...] = outgoing[...] + mapped
            carry_copy.start()

        high, low = pieces(mapped)
        for l in range(tiles):
            pick = spread[:, pl.ds(l * LANES, LANES)]
            wide = (jnp.dot(high, pick, preferred_element_type=jnp.float32)
                    + jnp.dot(low, pick, preferred_element_type=jnp.float32))
            for f in range(fields):
                part = wide[f * coarse_rows:(f + 1) * coarse_rows]
                for k in range(4):
                    at = pl.ds(PAD + k, coarse_rows, stride=4)
                    fine[f, l, at, :] = fine[f, l, at, :] + part
                send_out(f, l).start()

    for sends, _, copies in transfers:
        @pl.when(sends)
        def _(copies=copies):
            for copy in copies:
                copy.wait_send()

    @pl.when(n < slices - 1)
    def _():
        carry_copy.wait_send()

    for f in range(fields):
        for l in range(tiles):
            send_out(f, l).wait()


def local(sizes, starts, coarse_map, diffusivity):
    state, matrix = starts[0], coarse_map[0]
    fields, height, width = state.shape
    tiles = width // LANES
    full = height + 2 * PAD
    coarse = (fields * (height // 4), width // 4)
    f32, dma = jnp.float32, pltpu.SemaphoreType.DMA
    result = pl.pallas_call(
        functools.partial(kernel, sizes),
        out_shape=jax.ShapeDtypeStruct(state.shape, f32),
        in_specs=[
            pl.BlockSpec(memory_space=pl.ANY),
            pl.BlockSpec(memory_space=pl.ANY),
            pl.BlockSpec(memory_space=pltpu.SMEM),
        ],
        out_specs=pl.BlockSpec(memory_space=pl.ANY),
        scratch_shapes=[
            pltpu.VMEM((fields, tiles + 1, full, LANES), f32),
            pltpu.VMEM((fields, tiles + 1, full, LANES), f32),
            pltpu.VMEM((height, LANES), f32),
            pltpu.VMEM((full, LANES), f32),
            pltpu.VMEM((full, LANES), f32),
            pltpu.VMEM((full, LANES), f32),
            pltpu.VMEM((full, LANES), f32),
            pltpu.VMEM(matrix.shape, f32),
            pltpu.VMEM(coarse, f32),
            pltpu.VMEM((width, width // 4), jnp.bfloat16),
            pltpu.VMEM((width // 4, width), jnp.bfloat16),
            pltpu.VMEM(coarse, f32),
            pltpu.VMEM(coarse, f32),
            dma((tiles,)), dma,
            dma((2, tiles)), dma((2, tiles)), dma((2,)), dma((2,)), dma((2, 2)), dma((2, 2)),
            dma, dma, dma((fields, tiles)),
        ],
        compiler_params=pltpu.CompilerParams(
            collective_id=0, has_side_effects=True, vmem_limit_bytes=32 * 1024 * 1024),
        cost_estimate=pl.CostEstimate(
            flops=60 * state.size, bytes_accessed=12 * state.size, transcendentals=0),
    )(state, matrix, diffusivity)
    return result[None]


def solution(mesh):
    placed = (P("tm", None, "row", "gz"), P("tm", None, "row", "gz"), P())
    sizes = (mesh.shape["tm"], mesh.shape["gz"], mesh.shape["row"])
    return jax.shard_map(
        functools.partial(local, sizes), mesh=mesh, in_specs=placed,
        out_specs=P("tm", None, "row", "gz"), check_vma=False,
    )
```

```python
import functools

import jax
import jax.numpy as jnp
from jax import lax
from jax.experimental import pallas as pl
from jax.experimental.pallas import tpu as pltpu
from jax.sharding import PartitionSpec as P

FSTEPS = 4
TIME_STEP = 0.24
LANES = 128
PAD = 8
MESH = pl.DeviceIdType.MESH


def pieces(value):
    high = value.astype(jnp.bfloat16)
    low = (value - high.astype(jnp.float32)).astype(jnp.bfloat16)
    return high, low


def kernel(
    sizes, starts, coarse_map, diffusivity, out,
    state_a, state_b, packed, from_left, from_right, coef_a, coef_b, matrix,
    flux_east, flux_west, start_mean, gather, spread, outgoing, incoming,
    in_sem, map_sem, row_send, row_recv, col_send, col_recv, cor_send, cor_recv,
    carry_send, carry_recv, out_sem,
):
    slices, cols, rows = sizes
    fields, height, width = starts.shape
    tiles = width // LANES
    n, g, r = lax.axis_index("tm"), lax.axis_index("gz"), lax.axis_index("row")

    def load_tile(l):
        return pltpu.make_async_copy(
            starts.at[:, :, pl.ds(l * LANES, LANES)],
            state_a.at[:, l, pl.ds(PAD, height), :], in_sem.at[l])

    order = [0, tiles - 1] + list(range(1, tiles - 1))
    for l in order:
        load_tile(l).start()
    load_map = pltpu.make_async_copy(coarse_map, matrix, map_sem)
    load_map.start()

    up, down, left, right = r > 0, r < rows - 1, g > 0, g < cols - 1
    both = jnp.logical_and
    neighbours = [
        (up, {"row": r - 1}), (down, {"row": r + 1}),
        (left, {"gz": g - 1}), (right, {"gz": g + 1}),
        (both(up, left), {"row": r - 1, "gz": g - 1}),
        (both(up, right), {"row": r - 1, "gz": g + 1}),
        (both(down, left), {"row": r + 1, "gz": g - 1}),
        (both(down, right), {"row": r + 1, "gz": g + 1}),
        (n > 0, {"tm": n - 1}), (n < slices - 1, {"tm": n + 1}),
    ]
    barrier = pltpu.get_barrier_semaphore()
    present = 0
    for there, device in neighbours:
        present = present + there.astype(jnp.int32)

        @pl.when(there)
        def _(device=device):
            pl.semaphore_signal(barrier, inc=1, device_id=device, device_id_type=MESH)

    blank_rows = jnp.zeros((fields, tiles, PAD, LANES), jnp.float32)
    blank_tile = jnp.zeros((PAD, LANES), jnp.float32)
    bottom = PAD + height

    @pl.when(jnp.logical_not(up))
    def _():
        state_a[:, :tiles, 0:PAD, :] = blank_rows

    @pl.when(jnp.logical_not(down))
    def _():
        state_a[:, :tiles, bottom:, :] = blank_rows

    for ref, side in ((from_left, left), (from_right, right)):
        @pl.when(jnp.logical_not(both(side, up)))
        def _(ref=ref):
            ref[0:PAD, :] = blank_tile

        @pl.when(jnp.logical_not(both(side, down)))
        def _(ref=ref):
            ref[bottom:, :] = blank_tile

        @pl.when(jnp.logical_not(side))
        def _(ref=ref):
            ref[pl.ds(PAD, height), :] = jnp.zeros((height, LANES), jnp.float32)

    lane_all = lax.broadcasted_iota(jnp.int32, (height, LANES), 1)

    load_tile(0).wait()
    load_tile(tiles - 1).wait()
    pack = jnp.zeros((height, LANES), jnp.float32)
    for f in range(fields):
        edges = jnp.where(lane_all < 64, state_a[f, 0, pl.ds(PAD, height), :],
                          state_a[f, tiles - 1, pl.ds(PAD, height), :])
        pack = jnp.where(lane_all // 8 == f, pltpu.roll(edges, 8 * f + 4, 1), pack)
    packed[...] = pack

    pl.semaphore_wait(barrier, present)

    def row_copy(l, way):
        source = pl.ds(0, PAD) if way == 0 else pl.ds(height - PAD, PAD)
        target = pl.ds(bottom, PAD) if way == 0 else pl.ds(0, PAD)
        return pltpu.make_async_remote_copy(
            src_ref=starts.at[:, source, pl.ds(l * LANES, LANES)],
            dst_ref=state_a.at[:, l, target, :],
            send_sem=row_send.at[way, l], recv_sem=row_recv.at[way, l],
            device_id={"row": r - 1 if way == 0 else r + 1}, device_id_type=MESH)

    def col_copy(way):
        return pltpu.make_async_remote_copy(
            src_ref=packed,
            dst_ref=(from_right if way == 0 else from_left).at[pl.ds(PAD, height), :],
            send_sem=col_send.at[way], recv_sem=col_recv.at[way],
            device_id={"gz": g - 1 if way == 0 else g + 1}, device_id_type=MESH)

    def cor_copy(v, h):
        source = pl.ds(0, PAD) if v == 0 else pl.ds(height - PAD, PAD)
        target = pl.ds(bottom, PAD) if v == 0 else pl.ds(0, PAD)
        return pltpu.make_async_remote_copy(
            src_ref=packed.at[source, :],
            dst_ref=(from_right if h == 0 else from_left).at[target, :],
            send_sem=cor_send.at[v, h], recv_sem=cor_recv.at[v, h],
            device_id={"row": r - 1 if v == 0 else r + 1, "gz": g - 1 if h == 0 else g + 1},
            device_id_type=MESH)

    transfers = [
        (left, right, [col_copy(0)]),
        (right, left, [col_copy(1)]),
        (both(up, left), both(down, right), [cor_copy(0, 0)]),
        (both(up, right), both(down, left), [cor_copy(0, 1)]),
        (both(down, left), both(up, right), [cor_copy(1, 0)]),
        (both(down, right), both(up, left), [cor_copy(1, 1)]),
        (up, down, [row_copy(l, 0) for l in range(tiles)]),
        (down, up, [row_copy(l, 1) for l in range(tiles)]),
    ]
    for sends, _, copies in transfers:
        @pl.when(sends)
        def _(copies=copies):
            for copy in copies:
                copy.start()

    full = height + 2 * PAD
    grow = r * height - PAD + lax.broadcasted_iota(jnp.int32, (full, LANES), 0)
    radius = grow.astype(jnp.float32)
    inside = both(grow >= 0, grow < rows * height)
    coef_a[...] = jnp.where(inside, (radius + 1.0) / (radius + 0.5), 0.0)
    coef_b[...] = jnp.where(inside, radius / (radius + 0.5), 0.0)

    coarse_cols = width // 4
    fine_at = lax.broadcasted_iota(jnp.int32, (width, coarse_cols), 0)
    coarse_at = lax.broadcasted_iota(jnp.int32, (width, coarse_cols), 1)
    gather[...] = jnp.where(fine_at // 4 == coarse_at, 1.0, 0.0).astype(jnp.bfloat16)
    fine_at = lax.broadcasted_iota(jnp.int32, (coarse_cols, width), 1)
    coarse_at = lax.broadcasted_iota(jnp.int32, (coarse_cols, width), 0)
    spread[...] = jnp.where(fine_at // 4 == coarse_at, 1.0, 0.0).astype(jnp.bfloat16)

    coarse_rows = height // 4

    def restrict(ref):
        total = jnp.zeros((fields * coarse_rows, coarse_cols), jnp.float32)
        for l in range(tiles):
            sums = []
            for f in range(fields):
                part = [ref[f, l, pl.ds(PAD + k, coarse_rows, stride=4), :] for k in range(4)]
                sums.append((part[0] + part[1]) + (part[2] + part[3]))
            high, low = pieces(jnp.concatenate(sums, axis=0))
            pick = gather[pl.ds(l * LANES, LANES), :]
            total = total + jnp.dot(high, pick, preferred_element_type=jnp.float32)
            total = total + jnp.dot(low, pick, preferred_element_type=jnp.float32)
        return total * 0.0625

    for l in range(1, tiles - 1):
        load_tile(l).wait()

    @pl.when(n > 0)
    def _():
        start_mean[...] = restrict(state_a)

    for _, receives, copies in transfers:
        @pl.when(receives)
        def _(copies=copies):
            for copy in copies:
                copy.wait_recv()

    lane_full = lax.broadcasted_iota(jnp.int32, (full, LANES), 1)
    merged = jnp.where(lane_full % 8 < 4, from_left[...], from_right[...])
    edge = jnp.logical_or(lane_full < 4, lane_full >= LANES - 4)
    for f in range(fields):
        state_a[f, tiles] = jnp.where(edge, pltpu.roll(merged, LANES - 8 * f - 4, 1), 0.0)

    count = tiles + 1

    def fine_step(source, target, begin, height_now, block, wanted):
        for at in range(begin, begin + height_now, block):
            here = pl.ds(at, block)
            shape = (block, LANES)
            lane = lax.broadcasted_iota(jnp.int32, shape, 1)
            first, final = lane == 0, lane == LANES - 1
            speed = [jnp.tanh(source[1, l, here, :]) for l in range(count)]
            turned = [pltpu.roll(x, LANES - 1, 1) for x in speed]
            flux = [(0.0625 * TIME_STEP) * (speed[l] + jnp.where(
                final, turned[(l + 1) % count], turned[l])) for l in range(count)]
            turned = [pltpu.roll(x, 1, 1) for x in flux]
            for l in range(wanted):
                flux_east[l, here, :] = flux[l]
                flux_west[l, here, :] = jnp.where(first, turned[l - 1], turned[l])

        def body(f, _):
            rate = TIME_STEP * diffusivity[f]
            middle = 1.0 - 4.0 * rate
            for at in range(begin, begin + height_now, block):
                here = pl.ds(at, block)
                shape = (block, LANES)
                lane = lax.broadcasted_iota(jnp.int32, shape, 1)
                first, final = lane == 0, lane == LANES - 1
                a_f, b_f = rate * coef_a[here, :], rate * coef_b[here, :]
                for l in range(wanted):
                    center = source[f, l, here, :]
                    after = source[f, (l + 1) % count, here, :]
                    before = source[f, (l - 1) % count, here, :]
                    east = jnp.where(final, pltpu.roll(after, LANES - 1, 1),
                                     pltpu.roll(center, LANES - 1, 1))
                    west = jnp.where(first, pltpu.roll(before, 1, 1), pltpu.roll(center, 1, 1))
                    q, q_west = flux_east[l, here, :], flux_west[l, here, :]
                    new = (
                        center * (middle + (q_west - q)) + east * (rate - q)
                        + west * (rate + q_west)
                        + (a_f * source[f, l, pl.ds(at + 1, block), :]
                           + b_f * source[f, l, pl.ds(at - 1, block), :])
                    )
                    if l == tiles:
                        keep = jnp.logical_or(both(lane < 64, right), both(lane >= 64, left))
                        new = jnp.where(keep, new, 0.0)
                    target[f, l, here, :] = new
            return 0

        lax.fori_loop(0, fields, body, 0, unroll=True)

    source, target = state_a, state_b
    for turn in range(FSTEPS):
        if turn < FSTEPS - 1:
            fine_step(source, target, PAD - FSTEPS, height + 2 * FSTEPS, 24, count)
        else:
            fine_step(source, target, PAD, height, 16, tiles)
        source, target = target, source
    fine = source

    load_map.wait()

    carry_copy = pltpu.make_async_remote_copy(
        src_ref=outgoing, dst_ref=incoming, send_sem=carry_send, recv_sem=carry_recv,
        device_id={"tm": n + 1}, device_id_type=MESH)

    def send_out(f, l):
        return pltpu.make_async_copy(
            fine.at[f, l, pl.ds(PAD, height), :],
            out.at[f, :, pl.ds(l * LANES, LANES)], out_sem.at[f, l])

    @pl.when(n == 0)
    def _():
        for f in range(fields):
            for l in range(tiles):
                send_out(f, l).start()

        @pl.when(n < slices - 1)
        def _():
            outgoing[...] = restrict(fine)
            carry_copy.start()

    @pl.when(n > 0)
    def _():
        @pl.when(n < slices - 1)
        def _():
            outgoing[...] = restrict(fine)

        carry_copy.wait_recv()
        carry = incoming[...] - start_mean[...]
        mapped = []
        for f in range(fields):
            total = jnp.zeros((coarse_rows, coarse_cols), jnp.float32)
            for h in range(fields):
                total = total + matrix[f * fields + h] * carry[h * coarse_rows:(h + 1) * coarse_rows]
            mapped.append(total)
        mapped = jnp.concatenate(mapped, axis=0)

        @pl.when(n < slices - 1)
        def _():
            outgoing[...] = outgoing[...] + mapped
            carry_copy.start()

        high, low = pieces(mapped)
        for l in range(tiles):
            pick = spread[:, pl.ds(l * LANES, LANES)]
            wide = (jnp.dot(high, pick, preferred_element_type=jnp.float32)
                    + jnp.dot(low, pick, preferred_element_type=jnp.float32))
            for f in range(fields):
                part = wide[f * coarse_rows:(f + 1) * coarse_rows]
                for k in range(4):
                    at = pl.ds(PAD + k, coarse_rows, stride=4)
                    fine[f, l, at, :] = fine[f, l, at, :] + part
                send_out(f, l).start()

    for sends, _, copies in transfers:
        @pl.when(sends)
        def _(copies=copies):
            for copy in copies:
                copy.wait_send()

    @pl.when(n < slices - 1)
    def _():
        carry_copy.wait_send()

    for f in range(fields):
        for l in range(tiles):
            send_out(f, l).wait()


def local(sizes, starts, coarse_map, diffusivity):
    state, matrix = starts[0], coarse_map[0]
    fields, height, width = state.shape
    tiles = width // LANES
    full = height + 2 * PAD
    coarse = (fields * (height // 4), width // 4)
    f32, dma = jnp.float32, pltpu.SemaphoreType.DMA
    result = pl.pallas_call(
        functools.partial(kernel, sizes),
        out_shape=jax.ShapeDtypeStruct(state.shape, f32),
        in_specs=[
            pl.BlockSpec(memory_space=pltpu.HBM),
            pl.BlockSpec(memory_space=pltpu.HBM),
            pl.BlockSpec(memory_space=pltpu.SMEM),
        ],
        out_specs=pl.BlockSpec(memory_space=pltpu.HBM),
        scratch_shapes=[
            pltpu.VMEM((fields, tiles + 1, full, LANES), f32),
            pltpu.VMEM((fields, tiles + 1, full, LANES), f32),
            pltpu.VMEM((height, LANES), f32),
            pltpu.VMEM((full, LANES), f32),
            pltpu.VMEM((full, LANES), f32),
            pltpu.VMEM((full, LANES), f32),
            pltpu.VMEM((full, LANES), f32),
            pltpu.VMEM(matrix.shape, f32),
            pltpu.VMEM((tiles + 1, full, LANES), f32),
            pltpu.VMEM((tiles + 1, full, LANES), f32),
            pltpu.VMEM(coarse, f32),
            pltpu.VMEM((width, width // 4), jnp.bfloat16),
            pltpu.VMEM((width // 4, width), jnp.bfloat16),
            pltpu.VMEM(coarse, f32),
            pltpu.VMEM(coarse, f32),
            dma((tiles,)), dma,
            dma((2, tiles)), dma((2, tiles)), dma((2,)), dma((2,)), dma((2, 2)), dma((2, 2)),
            dma, dma, dma((fields, tiles)),
        ],
        compiler_params=pltpu.CompilerParams(
            collective_id=0, has_side_effects=True, vmem_limit_bytes=64 * 1024 * 1024),
        cost_estimate=pl.CostEstimate(
            flops=60 * state.size, bytes_accessed=12 * state.size, transcendentals=0),
    )(state, matrix, diffusivity)
    return result[None]


def solution(mesh):
    placed = (P("tm", None, "row", "gz"), P("tm", None, "row", "gz"), P())
    sizes = (mesh.shape["tm"], mesh.shape["gz"], mesh.shape["row"])
    return jax.shard_map(
        functools.partial(local, sizes), mesh=mesh, in_specs=placed,
        out_specs=P("tm", None, "row", "gz"), check_vma=False,
    )
```

```python
import functools

import jax
import jax.numpy as jnp
from jax import lax
from jax.experimental import pallas as pl
from jax.experimental.pallas import tpu as pltpu
from jax.sharding import PartitionSpec as P

FSTEPS = 4
TIME_STEP = 0.24
LANES = 128
PAD = 8
MESH = pl.DeviceIdType.MESH


def pieces(value):
    high = value.astype(jnp.bfloat16)
    low = (value - high.astype(jnp.float32)).astype(jnp.bfloat16)
    return high, low


def kernel(
    sizes, starts, coarse_map, diffusivity, out,
    state_a, state_b, state_c, packed, from_left, from_right, coef_a, coef_b, matrix,
    flux_east, flux_west, start_mean, gather, spread, outgoing, incoming,
    in_sem, map_sem, row_send, row_recv, col_send, col_recv, cor_send, cor_recv,
    carry_send, carry_recv, out_sem,
):
    slices, cols, rows = sizes
    fields, height, width = starts.shape
    tiles = width // LANES
    n, g, r = lax.axis_index("tm"), lax.axis_index("gz"), lax.axis_index("row")

    def load_tile(l):
        return pltpu.make_async_copy(
            starts.at[:, :, pl.ds(l * LANES, LANES)],
            state_a.at[:, l, pl.ds(PAD, height), :], in_sem.at[l])

    order = [0, tiles - 1] + list(range(1, tiles - 1))
    for l in order:
        load_tile(l).start()
    load_map = pltpu.make_async_copy(coarse_map, matrix, map_sem)
    load_map.start()

    up, down, left, right = r > 0, r < rows - 1, g > 0, g < cols - 1
    both = jnp.logical_and
    neighbours = [
        (up, {"row": r - 1}), (down, {"row": r + 1}),
        (left, {"gz": g - 1}), (right, {"gz": g + 1}),
        (both(up, left), {"row": r - 1, "gz": g - 1}),
        (both(up, right), {"row": r - 1, "gz": g + 1}),
        (both(down, left), {"row": r + 1, "gz": g - 1}),
        (both(down, right), {"row": r + 1, "gz": g + 1}),
        (n > 0, {"tm": n - 1}), (n < slices - 1, {"tm": n + 1}),
    ]
    barrier = pltpu.get_barrier_semaphore()
    present = 0
    for there, device in neighbours:
        present = present + there.astype(jnp.int32)

        @pl.when(there)
        def _(device=device):
            pl.semaphore_signal(barrier, inc=1, device_id=device, device_id_type=MESH)

    blank_rows = jnp.zeros((fields, tiles, PAD, LANES), jnp.float32)
    blank_tile = jnp.zeros((PAD, LANES), jnp.float32)
    bottom = PAD + height

    @pl.when(jnp.logical_not(up))
    def _():
        state_a[:, :tiles, 0:PAD, :] = blank_rows

    @pl.when(jnp.logical_not(down))
    def _():
        state_a[:, :tiles, bottom:, :] = blank_rows

    for ref, side in ((from_left, left), (from_right, right)):
        @pl.when(jnp.logical_not(both(side, up)))
        def _(ref=ref):
            ref[0:PAD, :] = blank_tile

        @pl.when(jnp.logical_not(both(side, down)))
        def _(ref=ref):
            ref[bottom:, :] = blank_tile

        @pl.when(jnp.logical_not(side))
        def _(ref=ref):
            ref[pl.ds(PAD, height), :] = jnp.zeros((height, LANES), jnp.float32)

    lane_all = lax.broadcasted_iota(jnp.int32, (height, LANES), 1)

    load_tile(0).wait()
    load_tile(tiles - 1).wait()
    pack = jnp.zeros((height, LANES), jnp.float32)
    for f in range(fields):
        edges = jnp.where(lane_all < 64, state_a[f, 0, pl.ds(PAD, height), :],
                          state_a[f, tiles - 1, pl.ds(PAD, height), :])
        pack = jnp.where(lane_all // 8 == f, pltpu.roll(edges, 8 * f + 4, 1), pack)
    packed[...] = pack

    pl.semaphore_wait(barrier, present)

    def row_copy(l, way):
        source = pl.ds(0, PAD) if way == 0 else pl.ds(height - PAD, PAD)
        target = pl.ds(bottom, PAD) if way == 0 else pl.ds(0, PAD)
        return pltpu.make_async_remote_copy(
            src_ref=starts.at[:, source, pl.ds(l * LANES, LANES)],
            dst_ref=state_a.at[:, l, target, :],
            send_sem=row_send.at[way, l], recv_sem=row_recv.at[way, l],
            device_id={"row": r - 1 if way == 0 else r + 1}, device_id_type=MESH)

    def col_copy(way):
        return pltpu.make_async_remote_copy(
            src_ref=packed,
            dst_ref=(from_right if way == 0 else from_left).at[pl.ds(PAD, height), :],
            send_sem=col_send.at[way], recv_sem=col_recv.at[way],
            device_id={"gz": g - 1 if way == 0 else g + 1}, device_id_type=MESH)

    def cor_copy(v, h):
        source = pl.ds(0, PAD) if v == 0 else pl.ds(height - PAD, PAD)
        target = pl.ds(bottom, PAD) if v == 0 else pl.ds(0, PAD)
        return pltpu.make_async_remote_copy(
            src_ref=packed.at[source, :],
            dst_ref=(from_right if h == 0 else from_left).at[target, :],
            send_sem=cor_send.at[v, h], recv_sem=cor_recv.at[v, h],
            device_id={"row": r - 1 if v == 0 else r + 1, "gz": g - 1 if h == 0 else g + 1},
            device_id_type=MESH)

    transfers = [
        (left, right, [col_copy(0)]),
        (right, left, [col_copy(1)]),
        (both(up, left), both(down, right), [cor_copy(0, 0)]),
        (both(up, right), both(down, left), [cor_copy(0, 1)]),
        (both(down, left), both(up, right), [cor_copy(1, 0)]),
        (both(down, right), both(up, left), [cor_copy(1, 1)]),
        (up, down, [row_copy(l, 0) for l in range(tiles)]),
        (down, up, [row_copy(l, 1) for l in range(tiles)]),
    ]
    for sends, _, copies in transfers:
        @pl.when(sends)
        def _(copies=copies):
            for copy in copies:
                copy.start()

    full = height + 2 * PAD
    shape = ((height + 2 * FSTEPS) // 8, 8, LANES)
    grow = (r * height - FSTEPS + lax.broadcasted_iota(jnp.int32, shape, 0)
            + shape[0] * lax.broadcasted_iota(jnp.int32, shape, 1))
    radius = grow.astype(jnp.float32)
    inside = both(grow >= 0, grow < rows * height)
    coef_a[...] = jnp.where(inside, (radius + 1.0) / (radius + 0.5), 0.0)
    coef_b[...] = jnp.where(inside, radius / (radius + 0.5), 0.0)

    coarse_cols = width // 4
    fine_at = lax.broadcasted_iota(jnp.int32, (width, coarse_cols), 0)
    coarse_at = lax.broadcasted_iota(jnp.int32, (width, coarse_cols), 1)
    gather[...] = jnp.where(fine_at // 4 == coarse_at, 1.0, 0.0).astype(jnp.bfloat16)
    fine_at = lax.broadcasted_iota(jnp.int32, (coarse_cols, width), 1)
    coarse_at = lax.broadcasted_iota(jnp.int32, (coarse_cols, width), 0)
    spread[...] = jnp.where(fine_at // 4 == coarse_at, 1.0, 0.0).astype(jnp.bfloat16)

    coarse_rows = height // 4

    def restrict(ref):
        total = jnp.zeros((fields * coarse_rows, coarse_cols), jnp.float32)
        for l in range(tiles):
            sums = []
            for f in range(fields):
                part = [ref[f, l, pl.ds(PAD + k, coarse_rows, stride=4), :] for k in range(4)]
                sums.append((part[0] + part[1]) + (part[2] + part[3]))
            high, low = pieces(jnp.concatenate(sums, axis=0))
            pick = gather[pl.ds(l * LANES, LANES), :]
            total = total + jnp.dot(high, pick, preferred_element_type=jnp.float32)
            total = total + jnp.dot(low, pick, preferred_element_type=jnp.float32)
        return total * 0.0625

    for l in range(1, tiles - 1):
        load_tile(l).wait()

    @pl.when(n > 0)
    def _():
        start_mean[...] = restrict(state_a)

    for _, receives, copies in transfers:
        @pl.when(receives)
        def _(copies=copies):
            for copy in copies:
                copy.wait_recv()

    lane_full = lax.broadcasted_iota(jnp.int32, (full, LANES), 1)
    merged = jnp.where(lane_full % 8 < 4, from_left[...], from_right[...])
    edge = jnp.logical_or(lane_full < 4, lane_full >= LANES - 4)
    for f in range(fields):
        state_a[f, tiles] = jnp.where(edge, pltpu.roll(merged, LANES - 8 * f - 4, 1), 0.0)

    count = tiles + 1
    groups = (height + 2 * FSTEPS) // 8
    base = PAD - FSTEPS
    lane = lax.broadcasted_iota(jnp.int32, (8, LANES), 1)
    first, final = lane == 0, lane == LANES - 1
    keep = jnp.logical_or(both(lane < 64, right), both(lane >= 64, left))

    def plain_load(f, l, v):
        return state_a[f, l, pl.ds(base + v, 8, stride=groups), :]

    def plain_store(f, l, v, value):
        state_a[f, l, pl.ds(base + v, 8, stride=groups), :] = value

    def turned_load(ref):
        def load(f, l, v):
            if v < 0:
                return pltpu.roll(ref[f, l, groups - 1], 1, 0)
            if v == groups:
                return pltpu.roll(ref[f, l, 0], 7, 0)
            return ref[f, l, v]
        return load

    def turned_store(ref):
        def store(f, l, v, value):
            ref[f, l, v] = value
        return store

    def fine_step(load, store, wanted):
        for v in range(groups):
            speed = [jnp.tanh(load(1, l, v)) for l in range(count)]
            turned = [pltpu.roll(x, LANES - 1, 1) for x in speed]
            flux = [(0.0625 * TIME_STEP) * (speed[l] + jnp.where(
                final, turned[(l + 1) % count], turned[l])) for l in range(count)]
            turned = [pltpu.roll(x, 1, 1) for x in flux]
            for l in range(wanted):
                flux_east[l, v] = flux[l]
                flux_west[l, v] = jnp.where(first, turned[l - 1], turned[l])

        def body(f, _):
            rate = TIME_STEP * diffusivity[f]
            middle = 1.0 - 4.0 * rate
            before = [load(f, l, -1) for l in range(wanted)]
            center = [load(f, l, 0) for l in range(count)]
            for v in range(groups):
                after = [load(f, l, v + 1) for l in range(count if v + 1 < groups else wanted)]
                a_f, b_f = rate * coef_a[v], rate * coef_b[v]
                east = [pltpu.roll(x, LANES - 1, 1) for x in center]
                west = [pltpu.roll(x, 1, 1) for x in center]
                for l in range(wanted):
                    q, q_west = flux_east[l, v], flux_west[l, v]
                    new = (
                        center[l] * (middle + (q_west - q))
                        + jnp.where(final, east[(l + 1) % count], east[l]) * (rate - q)
                        + jnp.where(first, west[l - 1], west[l]) * (rate + q_west)
                        + (a_f * after[l] + b_f * before[l])
                    )
                    if l == tiles:
                        new = jnp.where(keep, new, 0.0)
                    store(f, l, v, new)
                before, center = center[:wanted], after
            return 0

        lax.fori_loop(0, fields, body, 0, unroll=True)

    loads = [plain_load, turned_load(state_b), turned_load(state_c), turned_load(state_b)]
    stores = [turned_store(state_b), turned_store(state_c), turned_store(state_b), plain_store]
    for turn in range(FSTEPS):
        fine_step(loads[turn], stores[turn], count if turn < FSTEPS - 1 else tiles)
    fine = state_a

    load_map.wait()

    carry_copy = pltpu.make_async_remote_copy(
        src_ref=outgoing, dst_ref=incoming, send_sem=carry_send, recv_sem=carry_recv,
        device_id={"tm": n + 1}, device_id_type=MESH)

    def send_out(f, l):
        return pltpu.make_async_copy(
            fine.at[f, l, pl.ds(PAD, height), :],
            out.at[f, :, pl.ds(l * LANES, LANES)], out_sem.at[f, l])

    @pl.when(n == 0)
    def _():
        for f in range(fields):
            for l in range(tiles):
                send_out(f, l).start()

        @pl.when(n < slices - 1)
        def _():
            outgoing[...] = restrict(fine)
            carry_copy.start()

    @pl.when(n > 0)
    def _():
        @pl.when(n < slices - 1)
        def _():
            outgoing[...] = restrict(fine)

        carry_copy.wait_recv()
        carry = incoming[...] - start_mean[...]
        mapped = []
        for f in range(fields):
            total = jnp.zeros((coarse_rows, coarse_cols), jnp.float32)
            for h in range(fields):
                total = total + matrix[f * fields + h] * carry[h * coarse_rows:(h + 1) * coarse_rows]
            mapped.append(total)
        mapped = jnp.concatenate(mapped, axis=0)

        @pl.when(n < slices - 1)
        def _():
            outgoing[...] = outgoing[...] + mapped
            carry_copy.start()

        high, low = pieces(mapped)
        for l in range(tiles):
            pick = spread[:, pl.ds(l * LANES, LANES)]
            wide = (jnp.dot(high, pick, preferred_element_type=jnp.float32)
                    + jnp.dot(low, pick, preferred_element_type=jnp.float32))
            for f in range(fields):
                part = wide[f * coarse_rows:(f + 1) * coarse_rows]
                for k in range(4):
                    at = pl.ds(PAD + k, coarse_rows, stride=4)
                    fine[f, l, at, :] = fine[f, l, at, :] + part
                send_out(f, l).start()

    for sends, _, copies in transfers:
        @pl.when(sends)
        def _(copies=copies):
            for copy in copies:
                copy.wait_send()

    @pl.when(n < slices - 1)
    def _():
        carry_copy.wait_send()

    for f in range(fields):
        for l in range(tiles):
            send_out(f, l).wait()


def local(sizes, starts, coarse_map, diffusivity):
    state, matrix = starts[0], coarse_map[0]
    fields, height, width = state.shape
    tiles = width // LANES
    full, groups = height + 2 * PAD, (height + 2 * FSTEPS) // 8
    coarse = (fields * (height // 4), width // 4)
    f32, dma = jnp.float32, pltpu.SemaphoreType.DMA
    result = pl.pallas_call(
        functools.partial(kernel, sizes),
        out_shape=jax.ShapeDtypeStruct(state.shape, f32),
        in_specs=[
            pl.BlockSpec(memory_space=pltpu.HBM),
            pl.BlockSpec(memory_space=pltpu.HBM),
            pl.BlockSpec(memory_space=pltpu.SMEM),
        ],
        out_specs=pl.BlockSpec(memory_space=pltpu.HBM),
        scratch_shapes=[
            pltpu.VMEM((fields, tiles + 1, full, LANES), f32),
            pltpu.VMEM((fields, tiles + 1, groups, 8, LANES), f32),
            pltpu.VMEM((fields, tiles + 1, groups, 8, LANES), f32),
            pltpu.VMEM((height, LANES), f32),
            pltpu.VMEM((full, LANES), f32),
            pltpu.VMEM((full, LANES), f32),
            pltpu.VMEM((groups, 8, LANES), f32),
            pltpu.VMEM((groups, 8, LANES), f32),
            pltpu.VMEM(matrix.shape, f32),
            pltpu.VMEM((tiles + 1, groups, 8, LANES), f32),
            pltpu.VMEM((tiles + 1, groups, 8, LANES), f32),
            pltpu.VMEM(coarse, f32),
            pltpu.VMEM((width, width // 4), jnp.bfloat16),
            pltpu.VMEM((width // 4, width), jnp.bfloat16),
            pltpu.VMEM(coarse, f32),
            pltpu.VMEM(coarse, f32),
            dma((tiles,)), dma,
            dma((2, tiles)), dma((2, tiles)), dma((2,)), dma((2,)), dma((2, 2)), dma((2, 2)),
            dma, dma, dma((fields, tiles)),
        ],
        compiler_params=pltpu.CompilerParams(
            collective_id=0, has_side_effects=True, vmem_limit_bytes=64 * 1024 * 1024),
        cost_estimate=pl.CostEstimate(
            flops=60 * state.size, bytes_accessed=12 * state.size, transcendentals=0),
    )(state, matrix, diffusivity)
    return result[None]


def solution(mesh):
    placed = (P("tm", None, "row", "gz"), P("tm", None, "row", "gz"), P())
    sizes = (mesh.shape["tm"], mesh.shape["gz"], mesh.shape["row"])
    return jax.shard_map(
        functools.partial(local, sizes), mesh=mesh, in_specs=placed,
        out_specs=P("tm", None, "row", "gz"), check_vma=False,
    )
```

```python
import functools

import jax
import jax.numpy as jnp
from jax import lax
from jax.experimental import pallas as pl
from jax.experimental.pallas import tpu as pltpu
from jax.sharding import PartitionSpec as P

FSTEPS = 4
TIME_STEP = 0.24
LANES = 128
PAD = 8
MESH = pl.DeviceIdType.MESH


def pieces(value):
    high = value.astype(jnp.bfloat16)
    low = (value - high.astype(jnp.float32)).astype(jnp.bfloat16)
    return high, low


def kernel(
    sizes, starts, coarse_map, diffusivity_in, out,
    state_a, state_b, state_c, packed, from_left, from_right, coef_a, coef_b, matrix, diffusivity, tall,
    flux_east, flux_west, start_mean, gather, spread, outgoing, incoming,
    in_sem, map_sem, rate_sem, row_send, row_recv, col_send, col_recv, cor_send, cor_recv,
    carry_send, carry_recv,
):
    slices, cols, rows = sizes
    fields, height, width = starts.shape
    tiles = width // LANES
    n, g, r = lax.axis_index("tm"), lax.axis_index("gz"), lax.axis_index("row")

    def load_tile(l):
        return pltpu.make_async_copy(
            starts.at[:, :, pl.ds(l * LANES, LANES)],
            state_a.at[:, l, pl.ds(PAD, height), :], in_sem.at[l])

    order = [0, tiles - 1] + list(range(1, tiles - 1))
    for l in order:
        load_tile(l).start()
    load_map = pltpu.make_async_copy(coarse_map, matrix, map_sem)
    load_map.start()
    load_rate = pltpu.make_async_copy(diffusivity_in, diffusivity, rate_sem)
    load_rate.start()

    up, down, left, right = r > 0, r < rows - 1, g > 0, g < cols - 1
    both = jnp.logical_and
    neighbours = [
        (up, {"row": r - 1}), (down, {"row": r + 1}),
        (left, {"gz": g - 1}), (right, {"gz": g + 1}),
        (both(up, left), {"row": r - 1, "gz": g - 1}),
        (both(up, right), {"row": r - 1, "gz": g + 1}),
        (both(down, left), {"row": r + 1, "gz": g - 1}),
        (both(down, right), {"row": r + 1, "gz": g + 1}),
        (n > 0, {"tm": n - 1}), (n < slices - 1, {"tm": n + 1}),
    ]
    barrier = pltpu.get_barrier_semaphore()
    present = 0
    for there, device in neighbours:
        present = present + there.astype(jnp.int32)

        @pl.when(there)
        def _(device=device):
            pl.semaphore_signal(barrier, inc=1, device_id=device, device_id_type=MESH)

    blank_rows = jnp.zeros((fields, tiles, PAD, LANES), jnp.float32)
    blank_tile = jnp.zeros((PAD, LANES), jnp.float32)
    bottom = PAD + height

    @pl.when(jnp.logical_not(up))
    def _():
        state_a[:, :tiles, 0:PAD, :] = blank_rows

    @pl.when(jnp.logical_not(down))
    def _():
        state_a[:, :tiles, bottom:, :] = blank_rows

    for ref, side in ((from_left, left), (from_right, right)):
        @pl.when(jnp.logical_not(both(side, up)))
        def _(ref=ref):
            ref[0:PAD, :] = blank_tile

        @pl.when(jnp.logical_not(both(side, down)))
        def _(ref=ref):
            ref[bottom:, :] = blank_tile

        @pl.when(jnp.logical_not(side))
        def _(ref=ref):
            ref[pl.ds(PAD, height), :] = jnp.zeros((height, LANES), jnp.float32)

    lane_all = lax.broadcasted_iota(jnp.int32, (height, LANES), 1)

    load_tile(0).wait()
    load_tile(tiles - 1).wait()
    pack = jnp.zeros((height, LANES), jnp.float32)
    for f in range(fields):
        edges = jnp.where(lane_all < 64, state_a[f, 0, pl.ds(PAD, height), :],
                          state_a[f, tiles - 1, pl.ds(PAD, height), :])
        pack = jnp.where(lane_all // 8 == f, pltpu.roll(edges, 8 * f + 4, 1), pack)
    packed[...] = pack

    pl.semaphore_wait(barrier, present)

    def row_copy(l, way):
        source = pl.ds(0, FSTEPS) if way == 0 else pl.ds(height - FSTEPS, FSTEPS)
        target = pl.ds(bottom, FSTEPS) if way == 0 else pl.ds(PAD - FSTEPS, FSTEPS)
        return pltpu.make_async_remote_copy(
            src_ref=starts.at[:, source, pl.ds(l * LANES, LANES)],
            dst_ref=state_a.at[:, l, target, :],
            send_sem=row_send.at[way, l], recv_sem=row_recv.at[way, l],
            device_id={"row": r - 1 if way == 0 else r + 1}, device_id_type=MESH)

    def col_copy(way):
        return pltpu.make_async_remote_copy(
            src_ref=packed,
            dst_ref=(from_right if way == 0 else from_left).at[pl.ds(PAD, height), :],
            send_sem=col_send.at[way], recv_sem=col_recv.at[way],
            device_id={"gz": g - 1 if way == 0 else g + 1}, device_id_type=MESH)

    def cor_copy(v, h):
        source = pl.ds(0, PAD) if v == 0 else pl.ds(height - PAD, PAD)
        target = pl.ds(bottom, PAD) if v == 0 else pl.ds(0, PAD)
        return pltpu.make_async_remote_copy(
            src_ref=packed.at[source, :],
            dst_ref=(from_right if h == 0 else from_left).at[target, :],
            send_sem=cor_send.at[v, h], recv_sem=cor_recv.at[v, h],
            device_id={"row": r - 1 if v == 0 else r + 1, "gz": g - 1 if h == 0 else g + 1},
            device_id_type=MESH)

    transfers = [
        (left, right, [col_copy(0)]),
        (right, left, [col_copy(1)]),
        (both(up, left), both(down, right), [cor_copy(0, 0)]),
        (both(up, right), both(down, left), [cor_copy(0, 1)]),
        (both(down, left), both(up, right), [cor_copy(1, 0)]),
        (both(down, right), both(up, left), [cor_copy(1, 1)]),
        (up, down, [row_copy(l, 0) for l in range(tiles)]),
        (down, up, [row_copy(l, 1) for l in range(tiles)]),
    ]
    for sends, _, copies in transfers:
        @pl.when(sends)
        def _(copies=copies):
            for copy in copies:
                copy.start()

    full = height + 2 * PAD
    shape = ((height + 2 * FSTEPS) // 8, 8, LANES)
    grow = (r * height - FSTEPS + lax.broadcasted_iota(jnp.int32, shape, 0)
            + shape[0] * lax.broadcasted_iota(jnp.int32, shape, 1))
    radius = grow.astype(jnp.float32)
    inside = both(grow >= 0, grow < rows * height)
    coef_a[...] = jnp.where(inside, (radius + 1.0) / (radius + 0.5), 0.0)
    coef_b[...] = jnp.where(inside, radius / (radius + 0.5), 0.0)

    coarse_cols = width // 4
    fine_at = lax.broadcasted_iota(jnp.int32, (width, coarse_cols), 0)
    coarse_at = lax.broadcasted_iota(jnp.int32, (width, coarse_cols), 1)
    gather[...] = jnp.where(fine_at // 4 == coarse_at, 1.0, 0.0).astype(jnp.bfloat16)
    fine_at = lax.broadcasted_iota(jnp.int32, (coarse_cols, width), 1)
    coarse_at = lax.broadcasted_iota(jnp.int32, (coarse_cols, width), 0)
    spread[...] = jnp.where(fine_at // 4 == coarse_at, 1.0, 0.0).astype(jnp.bfloat16)

    coarse_rows = height // 4

    def restrict(ref):
        total = jnp.zeros((fields * coarse_rows, coarse_cols), jnp.float32)
        for l in range(tiles):
            sums = []
            for f in range(fields):
                part = [ref[f, l, pl.ds(PAD + k, coarse_rows, stride=4), :] for k in range(4)]
                sums.append((part[0] + part[1]) + (part[2] + part[3]))
            high, low = pieces(jnp.concatenate(sums, axis=0))
            pick = gather[pl.ds(l * LANES, LANES), :]
            total = total + jnp.dot(high, pick, preferred_element_type=jnp.float32)
            total = total + jnp.dot(low, pick, preferred_element_type=jnp.float32)
        return total * 0.0625

    for l in range(1, tiles - 1):
        load_tile(l).wait()

    @pl.when(n > 0)
    def _():
        start_mean[...] = restrict(state_a)

    for _, receives, copies in transfers:
        @pl.when(receives)
        def _(copies=copies):
            for copy in copies:
                copy.wait_recv()

    lane_full = lax.broadcasted_iota(jnp.int32, (full, LANES), 1)
    merged = jnp.where(lane_full % 8 < 4, from_left[...], from_right[...])
    edge = jnp.logical_or(lane_full < 4, lane_full >= LANES - 4)
    for f in range(fields):
        state_a[f, tiles] = jnp.where(edge, pltpu.roll(merged, LANES - 8 * f - 4, 1), 0.0)

    load_rate.wait()
    count = tiles + 1
    groups = (height + 2 * FSTEPS) // 8
    base = PAD - FSTEPS
    lane = lax.broadcasted_iota(jnp.int32, (8, LANES), 1)
    first, final = lane == 0, lane == LANES - 1
    keep = jnp.logical_or(both(lane < 64, right), both(lane >= 64, left))

    def plain_load(f, l, v):
        return state_a[f, l, pl.ds(base + v, 8, stride=groups), :]

    def plain_store(f, l, v, value):
        state_a[f, l, pl.ds(base + v, 8, stride=groups), :] = value

    def turned_load(ref):
        def load(f, l, v):
            if v < 0:
                return pltpu.roll(ref[f, l, groups - 1], 1, 0)
            if v == groups:
                return pltpu.roll(ref[f, l, 0], 7, 0)
            return ref[f, l, v]
        return load

    def turned_store(ref):
        def store(f, l, v, value):
            ref[f, l, v] = value
        return store

    def fine_step(load, store, wanted):
        for v in range(groups):
            speed = [jnp.tanh(load(1, l, v)) for l in range(count)]
            turned = [pltpu.roll(x, LANES - 1, 1) for x in speed]
            flux = [(0.0625 * TIME_STEP) * (speed[l] + jnp.where(
                final, turned[(l + 1) % count], turned[l])) for l in range(count)]
            turned = [pltpu.roll(x, 1, 1) for x in flux]
            for l in range(wanted):
                flux_east[l, v] = flux[l]
                flux_west[l, v] = jnp.where(first, turned[l - 1], turned[l])

        def body(f, _):
            rate = TIME_STEP * diffusivity[f]
            middle = 1.0 - 4.0 * rate
            before = [load(f, l, -1) for l in range(wanted)]
            center = [load(f, l, 0) for l in range(count)]
            for v in range(groups):
                after = [load(f, l, v + 1) for l in range(count if v + 1 < groups else wanted)]
                a_f, b_f = rate * coef_a[v], rate * coef_b[v]
                east = [pltpu.roll(x, LANES - 1, 1) for x in center]
                west = [pltpu.roll(x, 1, 1) for x in center]
                for l in range(wanted):
                    q, q_west = flux_east[l, v], flux_west[l, v]
                    new = (
                        center[l] * (middle + (q_west - q))
                        + jnp.where(final, east[(l + 1) % count], east[l]) * (rate - q)
                        + jnp.where(first, west[l - 1], west[l]) * (rate + q_west)
                        + (a_f * after[l] + b_f * before[l])
                    )
                    if l == tiles:
                        new = jnp.where(keep, new, 0.0)
                    store(f, l, v, new)
                before, center = center[:wanted], after
            return 0

        lax.fori_loop(0, fields, body, 0, unroll=True)

    loads = [plain_load, turned_load(state_b), turned_load(state_c), turned_load(state_b)]
    stores = [turned_store(state_b), turned_store(state_c), turned_store(state_b), plain_store]
    for turn in range(FSTEPS):
        fine_step(loads[turn], stores[turn], count if turn < FSTEPS - 1 else tiles)
    fine = state_a

    load_map.wait()

    carry_copy = pltpu.make_async_remote_copy(
        src_ref=outgoing, dst_ref=incoming, send_sem=carry_send, recv_sem=carry_recv,
        device_id={"tm": n + 1}, device_id_type=MESH)

    @pl.when(n == 0)
    def _():
        @pl.when(n < slices - 1)
        def _():
            outgoing[...] = restrict(fine)
            carry_copy.start()

        for f in range(fields):
            for l in range(tiles):
                out[f, :, pl.ds(l * LANES, LANES)] = fine[f, l, pl.ds(PAD, height), :]

    @pl.when(n > 0)
    def _():
        @pl.when(n < slices - 1)
        def _():
            outgoing[...] = restrict(fine)

        carry_copy.wait_recv()
        carry = incoming[...] - start_mean[...]
        mapped = []
        for f in range(fields):
            total = jnp.zeros((coarse_rows, coarse_cols), jnp.float32)
            for h in range(fields):
                total = total + matrix[f * fields + h] * carry[h * coarse_rows:(h + 1) * coarse_rows]
            mapped.append(total)
        mapped = jnp.concatenate(mapped, axis=0)

        @pl.when(n < slices - 1)
        def _():
            outgoing[...] = outgoing[...] + mapped
            carry_copy.start()

        for f in range(fields):
            for k in range(4):
                tall[pl.ds(f * height + k, coarse_rows, stride=4), :] = (
                    mapped[f * coarse_rows:(f + 1) * coarse_rows])
        for f in range(fields):
            high, low = pieces(tall[pl.ds(f * height, height), :])
            wide = (jnp.dot(high, spread[...], preferred_element_type=jnp.float32)
                    + jnp.dot(low, spread[...], preferred_element_type=jnp.float32))
            for l in range(tiles):
                at = pl.ds(l * LANES, LANES)
                out[f, :, at] = (fine[f, l, pl.ds(PAD, height), :]
                                 + wide[:, l * LANES:(l + 1) * LANES])

    for sends, _, copies in transfers:
        @pl.when(sends)
        def _(copies=copies):
            for copy in copies:
                copy.wait_send()

    @pl.when(n < slices - 1)
    def _():
        carry_copy.wait_send()


def local(sizes, starts, coarse_map, diffusivity):
    state, matrix = starts[0], coarse_map[0]
    fields, height, width = state.shape
    tiles = width // LANES
    full, groups = height + 2 * PAD, (height + 2 * FSTEPS) // 8
    coarse = (fields * (height // 4), width // 4)
    f32, dma = jnp.float32, pltpu.SemaphoreType.DMA
    result = pl.pallas_call(
        functools.partial(kernel, sizes),
        out_shape=pltpu.VMEM(state.shape, f32),
        in_specs=[
            pl.BlockSpec(memory_space=pltpu.HBM),
            pl.BlockSpec(memory_space=pltpu.HBM),
            pl.BlockSpec(memory_space=pltpu.HBM),
        ],
        out_specs=pl.BlockSpec(memory_space=pltpu.VMEM),
        scratch_shapes=[
            pltpu.VMEM((fields, tiles + 1, full, LANES), f32),
            pltpu.VMEM((fields, tiles + 1, groups, 8, LANES), f32),
            pltpu.VMEM((fields, tiles + 1, groups, 8, LANES), f32),
            pltpu.VMEM((height, LANES), f32),
            pltpu.VMEM((full, LANES), f32),
            pltpu.VMEM((full, LANES), f32),
            pltpu.VMEM((groups, 8, LANES), f32),
            pltpu.VMEM((groups, 8, LANES), f32),
            pltpu.VMEM(matrix.shape, f32),
            pltpu.SMEM((fields,), f32),
            pltpu.VMEM((fields * height, width // 4), f32),
            pltpu.VMEM((tiles + 1, groups, 8, LANES), f32),
            pltpu.VMEM((tiles + 1, groups, 8, LANES), f32),
            pltpu.VMEM(coarse, f32),
            pltpu.VMEM((width, width // 4), jnp.bfloat16),
            pltpu.VMEM((width // 4, width), jnp.bfloat16),
            pltpu.VMEM(coarse, f32),
            pltpu.VMEM(coarse, f32),
            dma((tiles,)), dma, dma,
            dma((2, tiles)), dma((2, tiles)), dma((2,)), dma((2,)), dma((2, 2)), dma((2, 2)),
            dma, dma,
        ],
        compiler_params=pltpu.CompilerParams(
            collective_id=0, has_side_effects=True, vmem_limit_bytes=56 * 1024 * 1024),
        cost_estimate=pl.CostEstimate(
            flops=60 * state.size, bytes_accessed=12 * state.size, transcendentals=0),
    )(state, matrix, diffusivity)
    return result[None]


def solution(mesh):
    placed = (P("tm", None, "row", "gz"), P("tm", None, "row", "gz"), P())
    sizes = (mesh.shape["tm"], mesh.shape["gz"], mesh.shape["row"])
    return jax.shard_map(
        functools.partial(local, sizes), mesh=mesh, in_specs=placed,
        out_specs=P("tm", None, "row", "gz"), check_vma=False,
    )
```

```python
import functools

import jax
import jax.numpy as jnp
from jax import lax
from jax.experimental import pallas as pl
from jax.experimental.pallas import tpu as pltpu
from jax.sharding import PartitionSpec as P

FSTEPS = 4
TIME_STEP = 0.24
LANES = 128
PAD = 8
MESH = pl.DeviceIdType.MESH


def pieces(value):
    high = value.astype(jnp.bfloat16)
    low = (value - high.astype(jnp.float32)).astype(jnp.bfloat16)
    return high, low


def kernel(
    sizes, starts, coarse_map, diffusivity_in, out,
    state_a, state_b, state_c, packed, from_left, from_right, coef_a, coef_b, matrix, diffusivity, tall,
    flux_east, flux_west, start_mean, gather, spread, outgoing, incoming,
    in_sem, map_sem, rate_sem, row_send, row_recv, col_send, col_recv, cor_send, cor_recv,
    carry_send, carry_recv,
):
    slices, cols, rows = sizes
    fields, height, width = starts.shape
    tiles = width // LANES
    n, g, r = lax.axis_index("tm"), lax.axis_index("gz"), lax.axis_index("row")

    def load_tile(l):
        return pltpu.make_async_copy(
            starts.at[:, :, pl.ds(l * LANES, LANES)],
            state_a.at[:, l, pl.ds(PAD, height), :], in_sem.at[l])

    order = [0, tiles - 1] + list(range(1, tiles - 1))
    for l in order:
        load_tile(l).start()
    load_map = pltpu.make_async_copy(coarse_map, matrix, map_sem)
    load_map.start()
    load_rate = pltpu.make_async_copy(diffusivity_in, diffusivity, rate_sem)
    load_rate.start()

    up, down, left, right = r > 0, r < rows - 1, g > 0, g < cols - 1
    both = jnp.logical_and
    neighbours = [
        (up, {"row": r - 1}), (down, {"row": r + 1}),
        (left, {"gz": g - 1}), (right, {"gz": g + 1}),
        (both(up, left), {"row": r - 1, "gz": g - 1}),
        (both(up, right), {"row": r - 1, "gz": g + 1}),
        (both(down, left), {"row": r + 1, "gz": g - 1}),
        (both(down, right), {"row": r + 1, "gz": g + 1}),
        (n > 0, {"tm": n - 1}), (n < slices - 1, {"tm": n + 1}),
    ]
    barrier = pltpu.get_barrier_semaphore()
    present = 0
    for there, device in neighbours:
        present = present + there.astype(jnp.int32)

        @pl.when(there)
        def _(device=device):
            pl.semaphore_signal(barrier, inc=1, device_id=device, device_id_type=MESH)

    blank_rows = jnp.zeros((fields, tiles, PAD, LANES), jnp.float32)
    blank_tile = jnp.zeros((PAD, LANES), jnp.float32)
    bottom = PAD + height

    @pl.when(jnp.logical_not(up))
    def _():
        state_a[:, :tiles, 0:PAD, :] = blank_rows

    @pl.when(jnp.logical_not(down))
    def _():
        state_a[:, :tiles, bottom:, :] = blank_rows

    for ref, side in ((from_left, left), (from_right, right)):
        @pl.when(jnp.logical_not(both(side, up)))
        def _(ref=ref):
            ref[0:PAD, :] = blank_tile

        @pl.when(jnp.logical_not(both(side, down)))
        def _(ref=ref):
            ref[bottom:, :] = blank_tile

        @pl.when(jnp.logical_not(side))
        def _(ref=ref):
            ref[pl.ds(PAD, height), :] = jnp.zeros((height, LANES), jnp.float32)

    lane_all = lax.broadcasted_iota(jnp.int32, (height, LANES), 1)

    pl.semaphore_wait(barrier, present)

    def row_copy(l, way):
        source = pl.ds(0, FSTEPS) if way == 0 else pl.ds(height - FSTEPS, FSTEPS)
        target = pl.ds(bottom, FSTEPS) if way == 0 else pl.ds(PAD - FSTEPS, FSTEPS)
        return pltpu.make_async_remote_copy(
            src_ref=starts.at[:, source, pl.ds(l * LANES, LANES)],
            dst_ref=state_a.at[:, l, target, :],
            send_sem=row_send.at[way, l], recv_sem=row_recv.at[way, l],
            device_id={"row": r - 1 if way == 0 else r + 1}, device_id_type=MESH)

    def col_copy(way):
        return pltpu.make_async_remote_copy(
            src_ref=packed,
            dst_ref=(from_right if way == 0 else from_left).at[pl.ds(PAD, height), :],
            send_sem=col_send.at[way], recv_sem=col_recv.at[way],
            device_id={"gz": g - 1 if way == 0 else g + 1}, device_id_type=MESH)

    def cor_copy(v, h):
        source = pl.ds(0, PAD) if v == 0 else pl.ds(height - PAD, PAD)
        target = pl.ds(bottom, PAD) if v == 0 else pl.ds(0, PAD)
        return pltpu.make_async_remote_copy(
            src_ref=packed.at[source, :],
            dst_ref=(from_right if h == 0 else from_left).at[target, :],
            send_sem=cor_send.at[v, h], recv_sem=cor_recv.at[v, h],
            device_id={"row": r - 1 if v == 0 else r + 1, "gz": g - 1 if h == 0 else g + 1},
            device_id_type=MESH)

    transfers = [
        (left, right, [col_copy(0)]),
        (right, left, [col_copy(1)]),
        (both(up, left), both(down, right), [cor_copy(0, 0)]),
        (both(up, right), both(down, left), [cor_copy(0, 1)]),
        (both(down, left), both(up, right), [cor_copy(1, 0)]),
        (both(down, right), both(up, left), [cor_copy(1, 1)]),
        (up, down, [row_copy(l, 0) for l in range(tiles)]),
        (down, up, [row_copy(l, 1) for l in range(tiles)]),
    ]
    def start(part):
        for sends, _, copies in part:
            @pl.when(sends)
            def _(copies=copies):
                for copy in copies:
                    copy.start()

    start(transfers[6:])

    load_tile(0).wait()
    load_tile(tiles - 1).wait()
    pack = jnp.zeros((height, LANES), jnp.float32)
    for f in range(fields):
        edges = jnp.where(lane_all < 64, state_a[f, 0, pl.ds(PAD, height), :],
                          state_a[f, tiles - 1, pl.ds(PAD, height), :])
        pack = jnp.where(lane_all // 8 == f, pltpu.roll(edges, 8 * f + 4, 1), pack)
    packed[...] = pack

    start(transfers[:6])

    full = height + 2 * PAD
    shape = ((height + 2 * FSTEPS) // 8, 8, LANES)
    grow = (r * height - FSTEPS + lax.broadcasted_iota(jnp.int32, shape, 0)
            + shape[0] * lax.broadcasted_iota(jnp.int32, shape, 1))
    radius = grow.astype(jnp.float32)
    inside = both(grow >= 0, grow < rows * height)
    coef_a[...] = jnp.where(inside, (radius + 1.0) / (radius + 0.5), 0.0)
    coef_b[...] = jnp.where(inside, radius / (radius + 0.5), 0.0)

    coarse_cols = width // 4
    fine_at = lax.broadcasted_iota(jnp.int32, (width, coarse_cols), 0)
    coarse_at = lax.broadcasted_iota(jnp.int32, (width, coarse_cols), 1)
    gather[...] = jnp.where(fine_at // 4 == coarse_at, 1.0, 0.0).astype(jnp.bfloat16)
    fine_at = lax.broadcasted_iota(jnp.int32, (coarse_cols, width), 1)
    coarse_at = lax.broadcasted_iota(jnp.int32, (coarse_cols, width), 0)
    spread[...] = jnp.where(fine_at // 4 == coarse_at, 1.0, 0.0).astype(jnp.bfloat16)

    coarse_rows = height // 4

    def restrict(ref):
        total = jnp.zeros((fields * coarse_rows, coarse_cols), jnp.float32)
        for l in range(tiles):
            sums = []
            for f in range(fields):
                part = [ref[f, l, pl.ds(PAD + k, coarse_rows, stride=4), :] for k in range(4)]
                sums.append((part[0] + part[1]) + (part[2] + part[3]))
            high, low = pieces(jnp.concatenate(sums, axis=0))
            pick = gather[pl.ds(l * LANES, LANES), :]
            total = total + jnp.dot(high, pick, preferred_element_type=jnp.float32)
            total = total + jnp.dot(low, pick, preferred_element_type=jnp.float32)
        return total * 0.0625

    for l in range(1, tiles - 1):
        load_tile(l).wait()

    @pl.when(n > 0)
    def _():
        start_mean[...] = restrict(state_a)

    for _, receives, copies in transfers:
        @pl.when(receives)
        def _(copies=copies):
            for copy in copies:
                copy.wait_recv()

    lane_full = lax.broadcasted_iota(jnp.int32, (full, LANES), 1)
    merged = jnp.where(lane_full % 8 < 4, from_left[...], from_right[...])
    edge = jnp.logical_or(lane_full < 4, lane_full >= LANES - 4)
    for f in range(fields):
        state_a[f, tiles] = jnp.where(edge, pltpu.roll(merged, LANES - 8 * f - 4, 1), 0.0)

    load_rate.wait()
    count = tiles + 1
    groups = (height + 2 * FSTEPS) // 8
    base = PAD - FSTEPS
    lane = lax.broadcasted_iota(jnp.int32, (8, LANES), 1)
    first, final = lane == 0, lane == LANES - 1
    keep = jnp.logical_or(both(lane < 64, right), both(lane >= 64, left))

    def plain_load(f, l, v):
        return state_a[f, l, pl.ds(base + v, 8, stride=groups), :]

    def plain_store(f, l, v, value):
        state_a[f, l, pl.ds(base + v, 8, stride=groups), :] = value

    def turned_load(ref):
        def load(f, l, v):
            if v < 0:
                return pltpu.roll(ref[f, l, groups - 1], 1, 0)
            if v == groups:
                return pltpu.roll(ref[f, l, 0], 7, 0)
            return ref[f, l, v]
        return load

    def turned_store(ref):
        def store(f, l, v, value):
            ref[f, l, v] = value
        return store

    def fine_step(load, store, wanted):
        for v in range(groups):
            speed = [jnp.tanh(load(1, l, v)) for l in range(count)]
            turned = [pltpu.roll(x, LANES - 1, 1) for x in speed]
            flux = [(0.0625 * TIME_STEP) * (speed[l] + jnp.where(
                final, turned[(l + 1) % count], turned[l])) for l in range(count)]
            turned = [pltpu.roll(x, 1, 1) for x in flux]
            for l in range(wanted):
                flux_east[l, v] = flux[l]
                flux_west[l, v] = jnp.where(first, turned[l - 1], turned[l])

        def body(f, _):
            rate = TIME_STEP * diffusivity[f]
            middle = 1.0 - 4.0 * rate
            before = [load(f, l, -1) for l in range(wanted)]
            center = [load(f, l, 0) for l in range(count)]
            for v in range(groups):
                after = [load(f, l, v + 1) for l in range(count if v + 1 < groups else wanted)]
                a_f, b_f = rate * coef_a[v], rate * coef_b[v]
                east = [pltpu.roll(x, LANES - 1, 1) for x in center]
                west = [pltpu.roll(x, 1, 1) for x in center]
                for l in range(wanted):
                    q, q_west = flux_east[l, v], flux_west[l, v]
                    new = (
                        center[l] * (middle + (q_west - q))
                        + jnp.where(final, east[(l + 1) % count], east[l]) * (rate - q)
                        + jnp.where(first, west[l - 1], west[l]) * (rate + q_west)
                        + (a_f * after[l] + b_f * before[l])
                    )
                    if l == tiles:
                        new = jnp.where(keep, new, 0.0)
                    store(f, l, v, new)
                before, center = center[:wanted], after
            return 0

        lax.fori_loop(0, fields, body, 0, unroll=True)

    loads = [plain_load, turned_load(state_b), turned_load(state_c), turned_load(state_b)]
    stores = [turned_store(state_b), turned_store(state_c), turned_store(state_b), plain_store]
    for turn in range(FSTEPS):
        fine_step(loads[turn], stores[turn], count if turn < FSTEPS - 1 else tiles)
    fine = state_a
    outgoing[...] = restrict(fine)

    carry_copy = pltpu.make_async_remote_copy(
        src_ref=outgoing, dst_ref=incoming, send_sem=carry_send, recv_sem=carry_recv,
        device_id={"tm": n + 1}, device_id_type=MESH)

    @pl.when(n == 0)
    def _():
        @pl.when(n < slices - 1)
        def _():
            carry_copy.start()

        for f in range(fields):
            for l in range(tiles):
                out[f, :, pl.ds(l * LANES, LANES)] = fine[f, l, pl.ds(PAD, height), :]
        load_map.wait()

    @pl.when(n > 0)
    def _():
        carry_copy.wait_recv()
        load_map.wait()
        carry = incoming[...] - start_mean[...]
        mapped = []
        for f in range(fields):
            total = jnp.zeros((coarse_rows, coarse_cols), jnp.float32)
            for h in range(fields):
                total = total + matrix[f * fields + h] * carry[h * coarse_rows:(h + 1) * coarse_rows]
            mapped.append(total)
        mapped = jnp.concatenate(mapped, axis=0)

        @pl.when(n < slices - 1)
        def _():
            outgoing[...] = outgoing[...] + mapped
            carry_copy.start()

        for f in range(fields):
            for k in range(4):
                tall[pl.ds(f * height + k, coarse_rows, stride=4), :] = (
                    mapped[f * coarse_rows:(f + 1) * coarse_rows])
        for f in range(fields):
            high, low = pieces(tall[pl.ds(f * height, height), :])
            wide = (jnp.dot(high, spread[...], preferred_element_type=jnp.float32)
                    + jnp.dot(low, spread[...], preferred_element_type=jnp.float32))
            for l in range(tiles):
                at = pl.ds(l * LANES, LANES)
                out[f, :, at] = (fine[f, l, pl.ds(PAD, height), :]
                                 + wide[:, l * LANES:(l + 1) * LANES])

    for sends, _, copies in transfers:
        @pl.when(sends)
        def _(copies=copies):
            for copy in copies:
                copy.wait_send()

    @pl.when(n < slices - 1)
    def _():
        carry_copy.wait_send()


def local(sizes, starts, coarse_map, diffusivity):
    state, matrix = starts[0], coarse_map[0]
    fields, height, width = state.shape
    tiles = width // LANES
    full, groups = height + 2 * PAD, (height + 2 * FSTEPS) // 8
    coarse = (fields * (height // 4), width // 4)
    f32, dma = jnp.float32, pltpu.SemaphoreType.DMA
    result = pl.pallas_call(
        functools.partial(kernel, sizes),
        out_shape=pltpu.VMEM(state.shape, f32),
        in_specs=[
            pl.BlockSpec(memory_space=pltpu.HBM),
            pl.BlockSpec(memory_space=pltpu.HBM),
            pl.BlockSpec(memory_space=pltpu.HBM),
        ],
        out_specs=pl.BlockSpec(memory_space=pltpu.VMEM),
        scratch_shapes=[
            pltpu.VMEM((fields, tiles + 1, full, LANES), f32),
            pltpu.VMEM((fields, tiles + 1, groups, 8, LANES), f32),
            pltpu.VMEM((fields, tiles + 1, groups, 8, LANES), f32),
            pltpu.VMEM((height, LANES), f32),
            pltpu.VMEM((full, LANES), f32),
            pltpu.VMEM((full, LANES), f32),
            pltpu.VMEM((groups, 8, LANES), f32),
            pltpu.VMEM((groups, 8, LANES), f32),
            pltpu.VMEM(matrix.shape, f32),
            pltpu.SMEM((fields,), f32),
            pltpu.VMEM((fields * height, width // 4), f32),
            pltpu.VMEM((tiles + 1, groups, 8, LANES), f32),
            pltpu.VMEM((tiles + 1, groups, 8, LANES), f32),
            pltpu.VMEM(coarse, f32),
            pltpu.VMEM((width, width // 4), jnp.bfloat16),
            pltpu.VMEM((width // 4, width), jnp.bfloat16),
            pltpu.VMEM(coarse, f32),
            pltpu.VMEM(coarse, f32),
            dma((tiles,)), dma, dma,
            dma((2, tiles)), dma((2, tiles)), dma((2,)), dma((2,)), dma((2, 2)), dma((2, 2)),
            dma, dma,
        ],
        compiler_params=pltpu.CompilerParams(
            collective_id=0, has_side_effects=True, vmem_limit_bytes=56 * 1024 * 1024),
        cost_estimate=pl.CostEstimate(
            flops=60 * state.size, bytes_accessed=12 * state.size, transcendentals=0),
    )(state, matrix, diffusivity)
    return result[None]


def solution(mesh):
    placed = (P("tm", None, "row", "gz"), P("tm", None, "row", "gz"), P())
    sizes = (mesh.shape["tm"], mesh.shape["gz"], mesh.shape["row"])
    return jax.shard_map(
        functools.partial(local, sizes), mesh=mesh, in_specs=placed,
        out_specs=P("tm", None, "row", "gz"), check_vma=False,
    )
```

```python
import functools

import jax
import jax.numpy as jnp
from jax import lax
from jax.experimental import pallas as pl
from jax.experimental.pallas import tpu as pltpu
from jax.sharding import PartitionSpec as P

FSTEPS = 4
TIME_STEP = 0.24
LANES = 128
PAD = 8
MESH = pl.DeviceIdType.MESH


def pieces(value):
    high = value.astype(jnp.bfloat16)
    low = (value - high.astype(jnp.float32)).astype(jnp.bfloat16)
    return high, low


def kernel(
    sizes, starts, coarse_map, diffusivity_in, out,
    state_a, state_b, state_c, packed, from_left, from_right, coef_a, coef_b, matrix, diffusivity, tall,
    flux_east, start_mean, gather, spread, outgoing, incoming,
    in_sem, map_sem, rate_sem, row_send, row_recv, col_send, col_recv, cor_send, cor_recv,
    carry_send, carry_recv,
):
    slices, cols, rows = sizes
    fields, height, width = starts.shape
    tiles = width // LANES
    n, g, r = lax.axis_index("tm"), lax.axis_index("gz"), lax.axis_index("row")

    def load_tile(l):
        return pltpu.make_async_copy(
            starts.at[:, :, pl.ds(l * LANES, LANES)],
            state_a.at[:, l, pl.ds(PAD, height), :], in_sem.at[l])

    order = [0, tiles - 1] + list(range(1, tiles - 1))
    for l in order:
        load_tile(l).start()
    load_map = pltpu.make_async_copy(coarse_map, matrix, map_sem)
    load_map.start()
    load_rate = pltpu.make_async_copy(diffusivity_in, diffusivity, rate_sem)
    load_rate.start()

    up, down, left, right = r > 0, r < rows - 1, g > 0, g < cols - 1
    both = jnp.logical_and
    neighbours = [
        (up, {"row": r - 1}), (down, {"row": r + 1}),
        (left, {"gz": g - 1}), (right, {"gz": g + 1}),
        (both(up, left), {"row": r - 1, "gz": g - 1}),
        (both(up, right), {"row": r - 1, "gz": g + 1}),
        (both(down, left), {"row": r + 1, "gz": g - 1}),
        (both(down, right), {"row": r + 1, "gz": g + 1}),
        (n > 0, {"tm": n - 1}), (n < slices - 1, {"tm": n + 1}),
    ]
    barrier = pltpu.get_barrier_semaphore()
    present = 0
    for there, device in neighbours:
        present = present + there.astype(jnp.int32)

        @pl.when(there)
        def _(device=device):
            pl.semaphore_signal(barrier, inc=1, device_id=device, device_id_type=MESH)

    blank_rows = jnp.zeros((fields, tiles, PAD, LANES), jnp.float32)
    blank_tile = jnp.zeros((PAD, LANES), jnp.float32)
    bottom = PAD + height

    @pl.when(jnp.logical_not(up))
    def _():
        state_a[:, :tiles, 0:PAD, :] = blank_rows

    @pl.when(jnp.logical_not(down))
    def _():
        state_a[:, :tiles, bottom:, :] = blank_rows

    for ref, side in ((from_left, left), (from_right, right)):
        @pl.when(jnp.logical_not(both(side, up)))
        def _(ref=ref):
            ref[0:PAD, :] = blank_tile

        @pl.when(jnp.logical_not(both(side, down)))
        def _(ref=ref):
            ref[bottom:, :] = blank_tile

        @pl.when(jnp.logical_not(side))
        def _(ref=ref):
            ref[pl.ds(PAD, height), :] = jnp.zeros((height, LANES), jnp.float32)

    lane_all = lax.broadcasted_iota(jnp.int32, (height, LANES), 1)

    load_tile(0).wait()
    load_tile(tiles - 1).wait()
    pack = jnp.zeros((height, LANES), jnp.float32)
    for f in range(fields):
        edges = jnp.where(lane_all < 64, state_a[f, 0, pl.ds(PAD, height), :],
                          state_a[f, tiles - 1, pl.ds(PAD, height), :])
        pack = jnp.where(lane_all // 8 == f, pltpu.roll(edges, 8 * f + 4, 1), pack)
    packed[...] = pack

    pl.semaphore_wait(barrier, present)

    def row_copy(l, way):
        source = pl.ds(0, FSTEPS) if way == 0 else pl.ds(height - FSTEPS, FSTEPS)
        target = pl.ds(bottom, FSTEPS) if way == 0 else pl.ds(PAD - FSTEPS, FSTEPS)
        return pltpu.make_async_remote_copy(
            src_ref=starts.at[:, source, pl.ds(l * LANES, LANES)],
            dst_ref=state_a.at[:, l, target, :],
            send_sem=row_send.at[way, l], recv_sem=row_recv.at[way, l],
            device_id={"row": r - 1 if way == 0 else r + 1}, device_id_type=MESH)

    def col_copy(way):
        return pltpu.make_async_remote_copy(
            src_ref=packed,
            dst_ref=(from_right if way == 0 else from_left).at[pl.ds(PAD, height), :],
            send_sem=col_send.at[way], recv_sem=col_recv.at[way],
            device_id={"gz": g - 1 if way == 0 else g + 1}, device_id_type=MESH)

    def cor_copy(v, h):
        source = pl.ds(0, PAD) if v == 0 else pl.ds(height - PAD, PAD)
        target = pl.ds(bottom, PAD) if v == 0 else pl.ds(0, PAD)
        return pltpu.make_async_remote_copy(
            src_ref=packed.at[source, :],
            dst_ref=(from_right if h == 0 else from_left).at[target, :],
            send_sem=cor_send.at[v, h], recv_sem=cor_recv.at[v, h],
            device_id={"row": r - 1 if v == 0 else r + 1, "gz": g - 1 if h == 0 else g + 1},
            device_id_type=MESH)

    transfers = [
        (left, right, [col_copy(0)]),
        (right, left, [col_copy(1)]),
        (both(up, left), both(down, right), [cor_copy(0, 0)]),
        (both(up, right), both(down, left), [cor_copy(0, 1)]),
        (both(down, left), both(up, right), [cor_copy(1, 0)]),
        (both(down, right), both(up, left), [cor_copy(1, 1)]),
        (up, down, [row_copy(l, 0) for l in range(tiles)]),
        (down, up, [row_copy(l, 1) for l in range(tiles)]),
    ]
    for sends, _, copies in transfers:
        @pl.when(sends)
        def _(copies=copies):
            for copy in copies:
                copy.start()

    full = height + 2 * PAD
    shape = ((height + 2 * FSTEPS) // 8, 8, LANES)
    grow = (r * height - FSTEPS + lax.broadcasted_iota(jnp.int32, shape, 0)
            + shape[0] * lax.broadcasted_iota(jnp.int32, shape, 1))
    radius = grow.astype(jnp.float32)
    inside = both(grow >= 0, grow < rows * height)
    coef_a[...] = jnp.where(inside, (radius + 1.0) / (radius + 0.5), 0.0)
    coef_b[...] = jnp.where(inside, radius / (radius + 0.5), 0.0)

    coarse_cols = width // 4
    fine_at = lax.broadcasted_iota(jnp.int32, (width, coarse_cols), 0)
    coarse_at = lax.broadcasted_iota(jnp.int32, (width, coarse_cols), 1)
    gather[...] = jnp.where(fine_at // 4 == coarse_at, 1.0, 0.0).astype(jnp.bfloat16)
    fine_at = lax.broadcasted_iota(jnp.int32, (coarse_cols, width), 1)
    coarse_at = lax.broadcasted_iota(jnp.int32, (coarse_cols, width), 0)
    spread[...] = jnp.where(fine_at // 4 == coarse_at, 1.0, 0.0).astype(jnp.bfloat16)

    coarse_rows = height // 4

    def restrict(ref):
        total = jnp.zeros((fields * coarse_rows, coarse_cols), jnp.float32)
        for l in range(tiles):
            sums = []
            for f in range(fields):
                part = [ref[f, l, pl.ds(PAD + k, coarse_rows, stride=4), :] for k in range(4)]
                sums.append((part[0] + part[1]) + (part[2] + part[3]))
            high, low = pieces(jnp.concatenate(sums, axis=0))
            pick = gather[pl.ds(l * LANES, LANES), :]
            total = total + jnp.dot(high, pick, preferred_element_type=jnp.float32)
            total = total + jnp.dot(low, pick, preferred_element_type=jnp.float32)
        return total * 0.0625

    for l in range(1, tiles - 1):
        load_tile(l).wait()

    @pl.when(n > 0)
    def _():
        start_mean[...] = restrict(state_a)

    for _, receives, copies in transfers:
        @pl.when(receives)
        def _(copies=copies):
            for copy in copies:
                copy.wait_recv()

    lane_full = lax.broadcasted_iota(jnp.int32, (full, LANES), 1)
    merged = jnp.where(lane_full % 8 < 4, from_left[...], from_right[...])
    edge = jnp.logical_or(lane_full < 4, lane_full >= LANES - 4)
    for f in range(fields):
        state_a[f, tiles] = jnp.where(edge, pltpu.roll(merged, LANES - 8 * f - 4, 1), 0.0)

    load_rate.wait()
    count = tiles + 1
    groups = (height + 2 * FSTEPS) // 8
    base = PAD - FSTEPS
    lane = lax.broadcasted_iota(jnp.int32, (8, LANES), 1)
    first, final = lane == 0, lane == LANES - 1
    keep = jnp.logical_or(both(lane < 64, right), both(lane >= 64, left))

    def plain_load(f, l, v):
        return state_a[f, l, pl.ds(base + v, 8, stride=groups), :]

    def plain_store(f, l, v, value):
        state_a[f, l, pl.ds(base + v, 8, stride=groups), :] = value

    def turned_load(ref):
        def load(f, l, v):
            if v < 0:
                return pltpu.roll(ref[f, l, groups - 1], 1, 0)
            if v == groups:
                return pltpu.roll(ref[f, l, 0], 7, 0)
            return ref[f, l, v]
        return load

    def turned_store(ref):
        def store(f, l, v, value):
            ref[f, l, v] = value
        return store

    def fine_step(load, store, wanted):
        for v in range(groups):
            speed = [jnp.tanh(load(1, l, v)) for l in range(count)]
            turned = [pltpu.roll(x, LANES - 1, 1) for x in speed]
            flux = [(0.0625 * TIME_STEP) * (speed[l] + jnp.where(
                final, turned[(l + 1) % count], turned[l])) for l in range(count)]
            for l in range(count):
                flux_east[l, v] = flux[l]

        def body(f, _):
            rate = TIME_STEP * diffusivity[f]
            middle = 1.0 - 2.0 * rate
            before = [load(f, l, -1) for l in range(wanted)]
            center = [load(f, l, 0) for l in range(count)]
            for v in range(groups):
                after = [load(f, l, v + 1) for l in range(count if v + 1 < groups else wanted)]
                a_f, b_f = rate * coef_a[v], rate * coef_b[v]
                east = [pltpu.roll(x, LANES - 1, 1) for x in center]
                face = []
                for l in range(count):
                    q = flux_east[l, v]
                    face.append(jnp.where(final, east[(l + 1) % count], east[l]) * (rate - q)
                                - center[l] * (rate + q))
                west = [pltpu.roll(x, 1, 1) for x in face]
                for l in range(wanted):
                    new = (
                        (center[l] * middle + (a_f * after[l] + b_f * before[l]))
                        + (face[l] - jnp.where(first, west[l - 1], west[l]))
                    )
                    if l == tiles:
                        new = jnp.where(keep, new, 0.0)
                    store(f, l, v, new)
                before, center = center[:wanted], after
            return 0

        lax.fori_loop(0, fields, body, 0, unroll=True)

    loads = [plain_load, turned_load(state_b), turned_load(state_c), turned_load(state_b)]
    stores = [turned_store(state_b), turned_store(state_c), turned_store(state_b), plain_store]
    for turn in range(FSTEPS):
        fine_step(loads[turn], stores[turn], count if turn < FSTEPS - 1 else tiles)
    fine = state_a

    load_map.wait()

    carry_copy = pltpu.make_async_remote_copy(
        src_ref=outgoing, dst_ref=incoming, send_sem=carry_send, recv_sem=carry_recv,
        device_id={"tm": n + 1}, device_id_type=MESH)

    @pl.when(n == 0)
    def _():
        @pl.when(n < slices - 1)
        def _():
            outgoing[...] = restrict(fine)
            carry_copy.start()

        for f in range(fields):
            for l in range(tiles):
                out[f, :, pl.ds(l * LANES, LANES)] = fine[f, l, pl.ds(PAD, height), :]

    @pl.when(n > 0)
    def _():
        @pl.when(n < slices - 1)
        def _():
            outgoing[...] = restrict(fine)

        carry_copy.wait_recv()
        carry = incoming[...] - start_mean[...]
        mapped = []
        for f in range(fields):
            total = jnp.zeros((coarse_rows, coarse_cols), jnp.float32)
            for h in range(fields):
                total = total + matrix[f * fields + h] * carry[h * coarse_rows:(h + 1) * coarse_rows]
            mapped.append(total)
        mapped = jnp.concatenate(mapped, axis=0)

        @pl.when(n < slices - 1)
        def _():
            outgoing[...] = outgoing[...] + mapped
            carry_copy.start()

        for f in range(fields):
            for k in range(4):
                tall[pl.ds(f * height + k, coarse_rows, stride=4), :] = (
                    mapped[f * coarse_rows:(f + 1) * coarse_rows])
        for f in range(fields):
            high, low = pieces(tall[pl.ds(f * height, height), :])
            wide = (jnp.dot(high, spread[...], preferred_element_type=jnp.float32)
                    + jnp.dot(low, spread[...], preferred_element_type=jnp.float32))
            for l in range(tiles):
                at = pl.ds(l * LANES, LANES)
                out[f, :, at] = (fine[f, l, pl.ds(PAD, height), :]
                                 + wide[:, l * LANES:(l + 1) * LANES])

    for sends, _, copies in transfers:
        @pl.when(sends)
        def _(copies=copies):
            for copy in copies:
                copy.wait_send()

    @pl.when(n < slices - 1)
    def _():
        carry_copy.wait_send()


def local(sizes, starts, coarse_map, diffusivity):
    state, matrix = starts[0], coarse_map[0]
    fields, height, width = state.shape
    tiles = width // LANES
    full, groups = height + 2 * PAD, (height + 2 * FSTEPS) // 8
    coarse = (fields * (height // 4), width // 4)
    f32, dma = jnp.float32, pltpu.SemaphoreType.DMA
    result = pl.pallas_call(
        functools.partial(kernel, sizes),
        out_shape=pltpu.VMEM(state.shape, f32),
        in_specs=[
            pl.BlockSpec(memory_space=pltpu.HBM),
            pl.BlockSpec(memory_space=pltpu.HBM),
            pl.BlockSpec(memory_space=pltpu.HBM),
        ],
        out_specs=pl.BlockSpec(memory_space=pltpu.VMEM),
        scratch_shapes=[
            pltpu.VMEM((fields, tiles + 1, full, LANES), f32),
            pltpu.VMEM((fields, tiles + 1, groups, 8, LANES), f32),
            pltpu.VMEM((fields, tiles + 1, groups, 8, LANES), f32),
            pltpu.VMEM((height, LANES), f32),
            pltpu.VMEM((full, LANES), f32),
            pltpu.VMEM((full, LANES), f32),
            pltpu.VMEM((groups, 8, LANES), f32),
            pltpu.VMEM((groups, 8, LANES), f32),
            pltpu.VMEM(matrix.shape, f32),
            pltpu.SMEM((fields,), f32),
            pltpu.VMEM((fields * height, width // 4), f32),
            pltpu.VMEM((tiles + 1, groups, 8, LANES), f32),
            pltpu.VMEM(coarse, f32),
            pltpu.VMEM((width, width // 4), jnp.bfloat16),
            pltpu.VMEM((width // 4, width), jnp.bfloat16),
            pltpu.VMEM(coarse, f32),
            pltpu.VMEM(coarse, f32),
            dma((tiles,)), dma, dma,
            dma((2, tiles)), dma((2, tiles)), dma((2,)), dma((2,)), dma((2, 2)), dma((2, 2)),
            dma, dma,
        ],
        compiler_params=pltpu.CompilerParams(
            collective_id=0, has_side_effects=True, vmem_limit_bytes=56 * 1024 * 1024),
        cost_estimate=pl.CostEstimate(
            flops=60 * state.size, bytes_accessed=12 * state.size, transcendentals=0),
    )(state, matrix, diffusivity)
    return result[None]


def solution(mesh):
    placed = (P("tm", None, "row", "gz"), P("tm", None, "row", "gz"), P())
    sizes = (mesh.shape["tm"], mesh.shape["gz"], mesh.shape["row"])
    return jax.shard_map(
        functools.partial(local, sizes), mesh=mesh, in_specs=placed,
        out_specs=P("tm", None, "row", "gz"), check_vma=False,
    )
```
